256 devices in a mesh: wave: 128 (over z, y, x), lev: 2 (over core).
Axes of the slice: x: 4, y: 4, z: 8, core: 2. Of those that a mesh axis runs over, the one named last changes fastest.
Arguments:
- fourier: bfloat16 [2, 2, 4, 2560, 1280], P(None, None, 'lev', 'wave'), may hold values from -6 to 6
- lat_rows: int32 [2560], replicated, may hold values from 0 to 2559, each once
- wave_slots: int32 [1280], replicated, may hold values from 0 to 1279, as said below
- pressure_balance_operator: float32 [4, 4], replicated, may hold values from -3 to 3
- depths: float32 [4], replicated, may hold values from 0.05 to 5
- vertical_modes: float32 [4, 4], replicated, may hold values from -3 to 3
- mode_projection: float32 [4, 4], replicated, may hold values from -3 to 3
- heat_link_operator: float32 [4, 4], replicated, may hold values from -3 to 3
Outputs:
- spectral_state: bfloat16 [1280, 2, 2, 4, 1280], P('wave', None, None, 'lev')
- grid_field: bfloat16 [2, 2, 4, 2560, 1280], P(None, None, 'lev', 'wave')
The draws below stay inside these ranges and needn't reach their ends.
Inputs may be any that keep to these rules, and one draw needn't show every extreme that they name: `lat_rows`: each latitude appears once. `wave_slots`: each wavenumber appears once; entry 2 i is below 640 and entry 2 i + 1 equals 1279 minus entry 2 i.
All inputs are finite; a program needn't handle non-finite values.
Results may differ from the reference program's by a relative error of at most 0.011.
Values may be sent and summed in bfloat16 or wider, within the bound.
A program may use at most 192 MiB of HBM per device.

```python
import math
import jax
import jax.numpy as jnp
from jax import lax

WAVES = 1280
NLAT = 2560
LEV = 4


def draw_wave_slots(key, part):
    key = jax.random.fold_in(key, 7)
    low_half = jax.random.permutation(key, WAVES // 2).astype(jnp.int32)
    return jnp.stack([low_half, WAVES - 1 - low_half], axis=1).reshape(WAVES)


def shard_levels(rng, extent, cuts, least, high):
    def one(dim, shards_of):
        draws = jax.random.uniform(jax.random.fold_in(jax.random.fold_in(rng, 6), dim), (shards_of,), jnp.float32, least / len(cuts), high / len(cuts))
        return jnp.repeat(jnp.exp(draws), extent[dim] // shards_of).reshape((-1,) + (1,) * (len(extent) - dim - 1))

    level = one(*cuts[0])
    for cut in cuts[1:]:
        level = level * one(*cut)
    return level


def gaussian(stream_key, shape, width, bound, split=(), kind=jnp.bfloat16):
    factor_of = shard_levels(stream_key, shape, split, -0.22, 0.18) if split else 1.0
    values = jax.random.normal(stream_key, shape, jnp.float32) * width * factor_of
    return jnp.minimum(jnp.maximum(values, -bound), bound).astype(kind)


def setup_inputs(seed: int = 0) -> dict:
    streams_of = jax.random.split(jax.random.key(seed), 9)
    fourier = gaussian(streams_of[0], (2, 2, LEV, NLAT, WAVES), 1.0, 6.0, ((2, 2), (3, 128)))
    lat_rows = jax.random.permutation(streams_of[1], NLAT).astype(jnp.int32)
    wave_slots = draw_wave_slots(jax.random.fold_in(streams_of[8], 71), 0)
    pressure_balance_operator = gaussian(streams_of[3], (LEV, LEV), LEV ** -0.5, 3.0, (), jnp.float32)
    depths = jnp.clip(jnp.exp(jax.random.uniform(streams_of[4], (LEV,), jnp.float32, math.log(0.05), math.log(5.0))), 0.05, 5.0)
    vertical_modes = gaussian(streams_of[5], (LEV, LEV), LEV ** -0.5, 3.0, (), jnp.float32)
    mode_projection = gaussian(streams_of[6], (LEV, LEV), LEV ** -0.5, 3.0, (), jnp.float32)
    heat_link_operator = gaussian(streams_of[7], (LEV, LEV), LEV ** -0.5, 3.0, (), jnp.float32)
    return dict(fourier=fourier, lat_rows=lat_rows, wave_slots=wave_slots, pressure_balance_operator=pressure_balance_operator, depths=depths, vertical_modes=vertical_modes, mode_projection=mode_projection, heat_link_operator=heat_link_operator)


def geometry(lat_count):
    hemisphere = lat_count // 2
    colatitude = jnp.pi * (jnp.arange(hemisphere, dtype=jnp.float32) + 0.5) / lat_count
    sine_row = jnp.sin(colatitude)
    return (jnp.cos(colatitude), sine_row, math.sqrt(math.pi / lat_count) * sine_row)

def legendre_tables(orders, cosine_row, sine_row, table_length, wave_count):
    degree_base = orders.astype(jnp.float32)[:, None]
    constant = 0.5 * math.log(math.pi)
    log_scale = 0.5 * (lax.lgamma(degree_base + 1.5) - lax.lgamma(degree_base + 1.0) - constant) + degree_base * jnp.log(sine_row)[None, :]
    former = jnp.zeros_like(log_scale)
    current = jnp.ones_like(log_scale)
    cosine_grid = cosine_row[None, :]

    def block_step(state_carry, block_start):
        former, current, log_scale = state_carry
        even_rows = []
        odd_rows = []
        for offset in range(64):
            degree = degree_base + (block_start + offset).astype(jnp.float32)
            entry_value = jnp.where(degree < wave_count, current * jnp.exp(log_scale), 0.0)
            if offset % 2 == 0:
                even_rows.append(entry_value.astype(jnp.bfloat16))
            else:
                odd_rows.append(entry_value.astype(jnp.bfloat16))
            next_degree = degree + 1.0
            grow_factor = jnp.sqrt((4.0 * next_degree * next_degree - 1.0) / (next_degree * next_degree - degree_base * degree_base))
            damp_factor = jnp.sqrt((degree * degree - degree_base * degree_base) / (4.0 * degree * degree - 1.0))
            following = grow_factor * (cosine_grid * current - damp_factor * former)
            former, current = (current, following)
            if offset % 8 == 7:
                magnitude = jnp.sqrt(former * former + current * current)
                former = former / magnitude
                current = current / magnitude
                log_scale = log_scale + jnp.log(magnitude)
        return ((former, current, log_scale), (jnp.stack(even_rows), jnp.stack(odd_rows)))
    block_starts = jnp.arange(table_length // 64, dtype=jnp.int32) * 64
    _, (even_table, odd_table) = lax.scan(block_step, (former, current, log_scale), block_starts)
    part_shape = (table_length // 2,) + log_scale.shape
    return (even_table.reshape(part_shape), odd_table.reshape(part_shape))

def coupling_table(orders, table_length, wave_count):
    degree = (orders[:, None] + jnp.arange(table_length, dtype=jnp.int32)[None, :]).astype(jnp.float32)
    return degree * (degree + 1.0) / float(wave_count * wave_count)

def vertical(harmonic_amplitudes, orders, matrices, wave_count):
    pressure_balance_operator, depths, vertical_modes, mode_projection, heat_link_operator = matrices
    maximal_legendre_order = lax.Precision.HIGHEST
    column_link_operator = coupling_table(orders, harmonic_amplitudes.shape[4], wave_count)[:, None, None, :]
    flow_spreading_grid = harmonic_amplitudes[:, :, 0]
    heat_grid_values = harmonic_amplitudes[:, :, 1]
    forcing_vector = flow_spreading_grid + column_link_operator * jnp.einsum('re,cney->cnry', pressure_balance_operator, heat_grid_values, precision=maximal_legendre_order)
    projected = jnp.einsum('re,cney->cnry', mode_projection, forcing_vector, precision=maximal_legendre_order)
    scaled = projected / (1.0 + column_link_operator * depths[None, None, :, None])
    flow_spreading_next = jnp.einsum('va,mrak->mrvk', vertical_modes, scaled, precision=maximal_legendre_order)
    heat_values_next = heat_grid_values - jnp.einsum('re,cney->cnry', heat_link_operator, flow_spreading_next, precision=maximal_legendre_order)
    return jnp.stack([flow_spreading_next, heat_values_next], axis=2)

def reference(fourier, lat_rows, wave_slots, pressure_balance_operator, depths, vertical_modes, mode_projection, heat_link_operator):
    wave_count = fourier.shape[4]
    lat_count = fourier.shape[3]
    hemisphere = lat_count // 2
    cosine_row, sine_row, weight_row = geometry(lat_count)
    position = jnp.zeros((lat_count,), jnp.int32).at[lat_rows].set(jnp.arange(lat_count, dtype=jnp.int32))
    north_rows = position[:hemisphere]
    south_rows = position[::-1][:hemisphere]
    widened = fourier.astype(jnp.float32)
    upper_half = jnp.take(widened, north_rows, axis=3)
    lower_half = jnp.take(widened, south_rows, axis=3)
    symmetric = ((upper_half + lower_half) * weight_row[:, None]).astype(jnp.bfloat16)
    antisymmetric = ((upper_half - lower_half) * weight_row[:, None]).astype(jnp.bfloat16)
    matrices = (pressure_balance_operator, depths, vertical_modes, mode_projection, heat_link_operator)
    group_size = 32

    def one_group(group_index):
        orders = group_index * group_size + jnp.arange(group_size, dtype=jnp.int32)
        sym_part = jnp.transpose(lax.dynamic_slice_in_dim(symmetric, group_index * group_size, group_size, 4), (4, 0, 1, 2, 3)).astype(jnp.float32)
        anti_part = jnp.transpose(lax.dynamic_slice_in_dim(antisymmetric, group_index * group_size, group_size, 4), (4, 0, 1, 2, 3)).astype(jnp.float32)
        even_table, odd_table = legendre_tables(orders, cosine_row, sine_row, wave_count, wave_count)
        even_wide = even_table.astype(jnp.float32)
        odd_wide = odd_table.astype(jnp.float32)
        even_part = jnp.einsum('mrfvh,kmh->mrfvk', sym_part, even_wide)
        odd_part = jnp.einsum('mrfvh,kmh->mrfvk', anti_part, odd_wide)
        harmonic_amplitudes = jnp.stack([even_part, odd_part], axis=-1).reshape(even_part.shape[:4] + (wave_count,))
        updated = vertical(harmonic_amplitudes, orders, matrices, wave_count).astype(jnp.bfloat16)
        updated_wide = updated.astype(jnp.float32)
        folded_sym = jnp.einsum('mrfvk,kmh->mrfvh', updated_wide[..., 0::2], even_wide)
        folded_anti = jnp.einsum('mrfvk,kmh->mrfvh', updated_wide[..., 1::2], odd_wide)
        return (updated, folded_sym, folded_anti)
    updated, folded_sym, folded_anti = lax.map(one_group, jnp.arange(wave_count // group_size, dtype=jnp.int32))
    updated = updated.reshape((wave_count,) + updated.shape[2:])
    folded_sym = folded_sym.reshape((wave_count,) + folded_sym.shape[2:])
    folded_anti = folded_anti.reshape((wave_count,) + folded_anti.shape[2:])
    spectral_state = jnp.take(updated, wave_slots, axis=0)
    mirror_index = jnp.minimum(lat_rows, lat_count - 1 - lat_rows)
    mirror_sign = jnp.where(lat_rows < hemisphere, 1.0, -1.0).astype(jnp.float32)
    row_values = jnp.take(folded_sym, mirror_index, axis=4) + mirror_sign * jnp.take(folded_anti, mirror_index, axis=4)
    grid_field = jnp.transpose((row_values * (1.0 / math.sqrt(wave_count))).astype(jnp.bfloat16), (1, 2, 3, 4, 0))
    return (spectral_state, grid_field)
```

```python
import functools
import math

import jax
import jax.numpy as jnp
import numpy as np
from jax import lax
from jax.experimental import pallas as pl
from jax.experimental.pallas import tpu as pltpu
from jax.sharding import PartitionSpec as P

MESH = pl.DeviceIdType.MESH
F32 = jnp.float32
BF16 = jnp.bfloat16

WAVES = 1280
NLAT = 2560
HEMI = NLAT // 2
NW = 128
ROWS = NLAT // NW
SLOTS = 5
TILES = HEMI // 128
CHAIN = 1296
BLOCKS = CHAIN // 16
PAD = 1408
ORDER = ((0, 1, 2, 3, 4), (6, 7, 8, 9, 5))
VMEM = 60 * 1024 * 1024


def constants():
    colat = np.pi * (np.arange(HEMI) + 0.5) / NLAT
    mixed = np.array(list(range(8)) + [8, 9] * 4)
    cosine = np.cos(colat).reshape(TILES, 128)[mixed].astype(np.float32)
    logsin = np.log(np.sin(colat)).reshape(TILES, 128)[mixed].astype(np.float32)
    weight = (math.sqrt(math.pi / NLAT) * np.sin(colat)).reshape(TILES, 128).T.astype(np.float32)
    start = np.array(
        [
            0.5 * (math.lgamma(m + 1.5) - math.lgamma(m + 1.0) - math.lgamma(1.5) - math.log(2.0))
            for m in range(WAVES)
        ],
        np.float32,
    )
    return cosine, logsin, weight, start


def iota(shape, axis):
    return lax.broadcasted_iota(jnp.int32, shape, axis)


def onehot(condition):
    return jnp.where(condition, 1.0, 0.0).astype(BF16)


def slot_onehot(core, slots_ref, hot):
    numbers = slots_ref[...]
    waves = iota((NW, WAVES), 1)
    for s in range(SLOTS):
        mine = jnp.where(
            core == 0,
            numbers[:, ORDER[0][s] : ORDER[0][s] + 1],
            numbers[:, ORDER[1][s] : ORDER[1][s] + 1],
        )
        hot[s * NW : (s + 1) * NW, :] = onehot(mine == waves)


def exchange(wave, core, send, land, own_sem, send_sem, recv_sem):
    own = pltpu.make_async_copy(send.at[wave], land.at[wave], own_sem)
    own.start()

    def start(step, _):
        target = lax.rem(wave + step, NW)
        pltpu.make_async_remote_copy(
            src_ref=send.at[target],
            dst_ref=land.at[wave],
            send_sem=send_sem,
            recv_sem=recv_sem,
            device_id=(target, core),
            device_id_type=MESH,
        ).start()
        return 0

    lax.fori_loop(1, NW, start, 0)

    def finish():
        own.wait()
        pltpu.make_async_copy(
            send.at[pl.ds(0, NW - 1)], land.at[pl.ds(0, NW - 1)], send_sem
        ).wait()
        pltpu.make_async_copy(
            send.at[pl.ds(0, NW - 1)], land.at[pl.ds(0, NW - 1)], recv_sem
        ).wait()

    return finish


def to_partner(wave, core, src, dst, send_sem, recv_sem):
    copy = pltpu.make_async_remote_copy(
        src_ref=src,
        dst_ref=dst,
        send_sem=send_sem,
        recv_sem=recv_sem,
        device_id=(wave, 1 - core),
        device_id_type=MESH,
    )
    copy.start()
    return copy


def forward_kernel(
    x_ref, slots_ref, out_ref, other, hot, rows, wide, send, land,
    pair_send, pair_recv, own_sem, send_sem, recv_sem,
):
    wave, core = lax.axis_index("wave"), lax.axis_index("lev")
    copy = to_partner(wave, core, x_ref, other, pair_send, pair_recv)
    slot_onehot(core, slots_ref, hot)
    copy.wait()
    for f in range(8):
        mine = x_ref[f].astype(F32)
        theirs = other[f].astype(F32)
        for v, value in (
            (0, jnp.where(core == 0, mine, theirs)),
            (1, jnp.where(core == 0, theirs, mine)),
        ):
            at = v * 64 + f * 8
            rows[at : at + 8, :] = value[0:8]
            rows[128 + at : 128 + at + 8, :] = value[8:16]
            rows[256 + at : 256 + at + 8, :] = jnp.concatenate(
                [value[16:20], jnp.zeros((4, WAVES), F32)], axis=0
            )
    arranged = lax.dot_general(
        hot[...],
        rows[...].astype(BF16),
        (((1,), (1,)), ((), ())),
        preferred_element_type=F32,
    )
    for c in range(3):
        for s in range(SLOTS):
            wide[pl.ds(c * 5 + s, NW, stride=16), :] = arranged[
                s * NW : (s + 1) * NW, c * 128 : (c + 1) * 128
            ]
    wide[pl.ds(15, NW, stride=16), :] = jnp.zeros((NW, 128), F32)
    send[...] = wide[...].astype(BF16).reshape(NW, 16, 128)
    exchange(wave, core, send, land, own_sem, send_sem, recv_sem)()
    out_ref[...] = land[...]


def transform_kernel(
    own_ref, start_ref, pressure_ref, depths_ref, modes_ref, project_ref, heat_ref,
    in_ref, lat_ref, cosine_ref, logsin_ref, weight_ref,
    out_ref, state_ref,
    coef_v, coef_s, table, block, wide, folded_in, folds, spec, turned, shuffle, grid, north_south,
    coef_sem,
):
    lane = iota((1, 128), 1)
    firsts = [own_ref[0], own_ref[2], own_ref[4]]
    seconds = [own_ref[1], own_ref[3], 0]
    begins = [(WAVES - firsts[c] + 15) // 16 * 16 for c in range(2)] + [CHAIN + 16]

    j = iota((8, PAD), 1)
    row = iota((8, PAD), 0)

    def per_chain(values):
        which = row % 4
        return jnp.where(which == 0, values[0], jnp.where(which == 1, values[1], values[2]))

    begin = per_chain(begins)
    second = j >= begin
    order = jnp.where(second, per_chain(seconds), per_chain(firsts))
    k = jnp.where(second, j - begin, j)
    n = (order + k).astype(F32)
    m = order.astype(F32)
    ok = (k >= 1) & (order + k < WAVES)
    grow = jnp.sqrt((4.0 * n * n - 1.0) / jnp.where(ok, n * n - m * m, 1.0))
    less = n - 1.0
    damp = jnp.sqrt(
        jnp.where(ok, jnp.maximum(less * less - m * m, 0.0), 0.0)
        / jnp.where(ok & (less > 0.0), 4.0 * less * less - 1.0, 1.0)
    )
    coef = jnp.where(ok, jnp.where(row < 4, grow, grow * damp), 0.0)
    coef_v[...] = coef
    coef_copy = pltpu.make_async_copy(coef_v, coef_s, coef_sem)
    coef_copy.start()

    source = iota((1, 1024), 1)
    source = (source % 128) // 16 * 128 + source % 16 * 8 + source // 128
    valid = iota((1, 1024), 1) % 128 < 80
    shuffle[...] = onehot(valid & (iota((640, 1024), 0) == source))
    wide[...] = in_ref[...].astype(F32).reshape(NW * 16, 128)
    lat = lat_ref[...]
    sign = jnp.where(lat < HEMI, 1.0, -1.0)
    for c in range(3):
        piece = jnp.concatenate(
            [wide[pl.ds(c * 5 + s, NW, stride=16), :].astype(BF16) for s in range(SLOTS)], axis=1
        )
        spread = jnp.dot(piece, shuffle[...], preferred_element_type=F32)
        for r in range(8 if c < 2 else 4):
            at = c * 8 + r
            part = spread[:, r * 128 : (r + 1) * 128]
            folded_in[at * NW : (at + 1) * NW, 0:128] = part.astype(BF16)
            folded_in[at * NW : (at + 1) * NW, 128:256] = (part * sign[:, at : at + 1]).astype(BF16)

    mirror = jnp.minimum(lat, NLAT - 1 - lat)
    mirror_rows = jnp.transpose(
        jnp.concatenate([mirror.astype(F32), jnp.zeros((NW, 128 - ROWS), F32)], axis=1)
    ).astype(jnp.int32)
    mirror_line = jnp.concatenate([mirror_rows[r : r + 1, :] for r in range(ROWS)], axis=1)

    def fold(t, _):
        hot = onehot(mirror_line == iota((256, NLAT), 0) + t * 256)
        total = jnp.dot(hot, folded_in[...], preferred_element_type=F32)
        at = pl.multiple_of(t * 256, 256)
        folds[pl.ds(at, 256), :] = total
        return 0

    lax.fori_loop(0, HEMI // 256, fold, 0)
    fold_total = [
        (folds[t * 128 : (t + 1) * 128, :] * weight_ref[:, t : t + 1]).astype(BF16)
        for t in range(TILES)
    ]
    for t in range(TILES):
        north_south[t * 128 : (t + 1) * 128, :] = fold_total[t]

    coef_copy.wait()
    cosine = [cosine_ref[0:8, :]] * 3 + [cosine_ref[8:16, :]]
    logsin = [logsin_ref[0:8, :]] * 3 + [logsin_ref[8:16, :]]
    sub = iota((8, 128), 0)

    def spread_rows(values):
        mixed = jnp.where(sub < 2, values[0], jnp.where(sub < 4, values[1], values[2]))
        return [values[0], values[1], values[2], mixed]

    def make(b, carry):
        current, former, scale = carry
        at_begin = [b * 16 == begins[c] for c in range(3)]
        wave_number = [
            jnp.where(at_begin[c], seconds[c], firsts[c]) for c in range(3)
        ]
        base = spread_rows([start_ref[w] for w in wave_number])
        degree = spread_rows([w.astype(F32) for w in wave_number])
        reset = spread_rows(
            [jnp.where((b == 0) | at_begin[c], 1.0, 0.0) for c in range(3)]
        )
        next_current, next_former, next_scale, factor = [], [], [], []
        for v in range(4):
            size = jnp.maximum(
                jnp.maximum(jnp.abs(current[v]), jnp.abs(former[v])), 1e-30
            )
            inverse = 1.0 / size
            again = reset[v] > 0.5
            if v < 3:
                again = jnp.broadcast_to(reset[v], (8, 128)) > 0.5
            next_current.append(jnp.where(again, 1.0, current[v] * inverse))
            next_former.append(jnp.where(again, 0.0, former[v] * inverse))
            next_scale.append(
                jnp.where(again, base[v] + degree[v] * logsin[v], scale[v] + jnp.log(size))
            )
            factor.append(jnp.exp(next_scale[v]))
        current, former = next_current, next_former
        for o in range(16):
            for v in range(4):
                block[o * 32 + v * 8 : o * 32 + v * 8 + 8, :] = current[v] * factor[v]
            at = b * 16 + o + 1
            grow = spread_rows([coef_s[c, at] for c in range(3)])
            damp = spread_rows([coef_s[4 + c, at] for c in range(3)])
            following = [
                (cosine[v] * grow[v]) * current[v] - damp[v] * former[v] for v in range(4)
            ]
            former, current = current, following
        at = pl.multiple_of(b * 16, 16)
        for c in range(3):
            for t in range(TILES):
                line = c * 8 + t if t < 8 else 24 + 2 * c + t - 8
                table[c, pl.ds(at, 16), t * 128 : (t + 1) * 128] = block[
                    pl.ds(line, 16, stride=32), :
                ].astype(BF16)
        return (tuple(current), tuple(former), tuple(next_scale))

    zeros = tuple(jnp.zeros((8, 128), F32) for _ in range(4))
    lax.fori_loop(0, BLOCKS, make, (zeros, zeros, zeros))

    chain_of = lane // 32

    def lanes(values):
        return jnp.where(chain_of == 0, values[0], jnp.where(chain_of == 1, values[1], values[2]))

    is_second = (lane // 16) % 2 == 1
    lane_begin = lanes(begins)
    offset = jnp.where(is_second, lanes(seconds) - lane_begin, lanes(firsts))
    level = (lane // 8) % 2 * 2 + lane % 2
    field = (lane // 2) % 2
    depth = jnp.zeros((1, 128), F32)
    for a in range(4):
        depth = jnp.where(level == a, depths_ref[a], depth)
    across, down = iota((128, 128), 1), iota((128, 128), 0)
    same = (across // 16 == down // 16) & ((across // 4) % 2 == (down // 4) % 2)
    level_to, level_from = (across // 8) % 2 * 2 + across % 2, (down // 8) % 2 * 2 + down % 2
    field_to, field_from = (across // 2) % 2, (down // 2) % 2

    def matrix(entry, to, of):
        total = jnp.zeros((128, 128), F32)
        for a in range(4):
            for b in range(4):
                total = jnp.where((level_to == a) & (level_from == b), entry(a, b), total)
        return jnp.where(same & (field_to == to) & (field_from == of), total, 0.0)

    def product(one, two):
        return lambda a, b: sum(one[a, e] * two[e, b] for e in range(4))

    first_matrix = jnp.concatenate(
        [
            matrix(lambda a, b: project_ref[a, b], 0, 0),
            matrix(product(project_ref, pressure_ref), 0, 1),
        ],
        axis=1,
    )
    second_matrix = matrix(lambda a, b: modes_ref[a, b], 0, 0) - matrix(
        product(heat_ref, modes_ref), 1, 0
    )
    turned[:, CHAIN - 16 : PAD] = jnp.zeros((128, PAD - CHAIN + 16), F32)
    spec[CHAIN - 16 : PAD, :] = jnp.zeros((PAD - CHAIN + 16, 128), F32)
    step_rows = CHAIN // 3

    def solve(q, _):
        at = pl.multiple_of(q * step_rows, 16)
        j = iota((step_rows, 128), 0) + at
        parts = []
        for c in range(3):
            both = jnp.dot(
                table[c, pl.ds(at, step_rows), :], north_south[...], preferred_element_type=F32
            )
            parts.append(jnp.where(j % 2 == 0, both[:, 0:128], both[:, 128:256]))
        spectrum = jnp.where(chain_of == 0, parts[0], jnp.where(chain_of == 1, parts[1], parts[2]))
        spectrum = jnp.where((j >= lane_begin) == is_second, spectrum, 0.0)
        n = (j + offset).astype(F32)
        coupling = n * (n + 1.0) * (1.0 / float(WAVES * WAVES))
        mixed = jnp.dot(
            spectrum, first_matrix, precision=lax.Precision.HIGHEST, preferred_element_type=F32
        )
        scaled = (mixed[:, 0:128] + coupling * mixed[:, 128:256]) / (1.0 + coupling * depth)
        updated = jnp.dot(
            scaled, second_matrix, precision=lax.Precision.HIGHEST, preferred_element_type=F32
        ) + jnp.where(field == 1, spectrum, 0.0)
        spec[pl.ds(at, step_rows), :] = updated.astype(BF16).astype(F32)
        return 0

    lax.fori_loop(0, 3, solve, 0)
    for t in range(PAD // 128):
        turned[:, t * 128 : (t + 1) * 128] = jnp.transpose(spec[t * 128 : (t + 1) * 128, :])
    for s in range(SLOTS):
        for v in range(2):
            value = turned[s * 16 + v * 8 : s * 16 + v * 8 + 8, :]
            if s % 2 == 1:
                value = pltpu.roll(value, PAD - begins[s // 2], 1)
            state_ref[v, s] = value[:, 0:WAVES].astype(BF16)

    even = iota((1, CHAIN), 1) % 2 == 0
    inverse_scale = 1.0 / math.sqrt(WAVES)
    for c in range(3):
        state = turned[c * 32 : c * 32 + 32, 0:CHAIN]
        left = jnp.concatenate(
            [jnp.where(even, state, 0.0), jnp.where(even, 0.0, state)], axis=0
        ).astype(BF16)
        for t in range(HEMI // 256):
            both = jnp.dot(
                left, table[c, :, t * 256 : (t + 1) * 256], preferred_element_type=F32
            )
            for u in range(2):
                sym = both[0:32, u * 128 : (u + 1) * 128]
                anti = both[32:64, u * 128 : (u + 1) * 128]
                at = t * 256 + u * 128
                wide[at : at + 128, c * 32 : c * 32 + 32] = jnp.transpose(
                    (sym + anti) * inverse_scale
                )
                folds[at : at + 128, c * 32 : c * 32 + 32] = jnp.transpose(
                    (sym - anti) * inverse_scale
                )
    used = lane < 80
    north_south[:, 0:128] = jnp.where(used, wide[0:HEMI, :], 0.0).astype(BF16)
    north_south[:, 128:256] = jnp.where(used, folds[:, 0:128], 0.0).astype(BF16)

    latitudes = iota((NW, HEMI), 1)
    for q in range(5):
        hot = jnp.concatenate(
            [onehot(mirror[:, r : r + 1] == latitudes) for r in range(q * 4, q * 4 + 4)], axis=0
        )
        both = jnp.dot(hot, north_south[...], preferred_element_type=F32)
        for u in range(4):
            r = q * 4 + u
            part = both[u * NW : (u + 1) * NW]
            grid[:, r * 128 : (r + 1) * 128] = jnp.where(
                sign[:, r : r + 1] > 0.0, part[:, 0:128], part[:, 128:256]
            ).astype(BF16)
    grid[:, ROWS * 128 : 24 * 128] = jnp.zeros((NW, 512), BF16)
    for c in range(3):
        piece = lax.dot_general(
            grid[:, c * 1024 : (c + 1) * 1024],
            shuffle[...],
            (((1,), (1,)), ((), ())),
            preferred_element_type=F32,
        )
        for s in range(SLOTS):
            wide[pl.ds(c * 5 + s, NW, stride=16), :] = piece[:, s * 128 : (s + 1) * 128]
    wide[pl.ds(15, NW, stride=16), :] = jnp.zeros((NW, 128), F32)
    out_ref[...] = wide[...].astype(BF16).reshape(NW, 16, 128)


def backward_kernel(
    in_ref, state_ref, slots_ref, spectral_ref, grid_ref,
    hot, wide, land, state_other, half, half_other,
    own_sem, send_sem, recv_sem, state_send, state_recv, pair_send, pair_recv,
):
    wave, core = lax.axis_index("wave"), lax.axis_index("lev")
    state_copy = to_partner(wave, core, state_ref.at[1 - core], state_other, state_send, state_recv)
    finish = exchange(wave, core, in_ref, land, own_sem, send_sem, recv_sem)
    slot_onehot(core, slots_ref, hot)
    state_copy.wait()
    for s in range(SLOTS):
        mine = jnp.where(core == 0, state_ref[0, s].astype(F32), state_ref[1, s].astype(F32))
        theirs = state_other[s].astype(F32)
        spectral_ref[ORDER[0][s]] = jnp.where(core == 0, mine, theirs).astype(BF16)
        spectral_ref[ORDER[1][s]] = jnp.where(core == 0, theirs, mine).astype(BF16)
    finish()
    wide[...] = land[...].astype(F32).reshape(NW * 16, 128)
    left = jnp.concatenate(
        [
            jnp.concatenate(
                [
                    jnp.transpose(wide[pl.ds(c * 5 + s, NW, stride=16), :])
                    for s in range(SLOTS)
                ],
                axis=1,
            )
            for c in range(3)
        ],
        axis=0,
    ).astype(BF16)
    rows = jnp.dot(left, hot[...], preferred_element_type=F32)
    kept = []
    for f in range(8):
        values = []
        for v in range(2):
            at = v * 64 + f * 8
            values.append(
                jnp.concatenate(
                    [rows[at : at + 8], rows[128 + at : 136 + at], rows[256 + at : 260 + at]],
                    axis=0,
                )
            )
        half[f] = jnp.where(core == 0, values[1], values[0]).astype(BF16)
        kept.append(jnp.where(core == 0, values[0], values[1]))
    copy = to_partner(wave, core, half, half_other, pair_send, pair_recv)
    copy.wait()
    for f in range(8):
        grid_ref[f] = (kept[f] + half_other[f].astype(F32)).astype(BF16)


def vmem():
    return pl.BlockSpec(memory_space=pltpu.VMEM)


def smem():
    return pl.BlockSpec(memory_space=pltpu.SMEM)


DMA = pltpu.SemaphoreType.DMA


def forward(x, slots):
    return pl.pallas_call(
        forward_kernel,
        out_shape=jax.ShapeDtypeStruct((NW, 16, 128), BF16),
        in_specs=[vmem(), vmem()],
        out_specs=vmem(),
        scratch_shapes=[
            pltpu.VMEM((8, ROWS, WAVES), BF16),
            pltpu.VMEM((SLOTS * NW, WAVES), BF16),
            pltpu.VMEM((384, WAVES), F32),
            pltpu.VMEM((NW * 16, 128), F32),
            pltpu.VMEM((NW, 16, 128), BF16),
            pltpu.VMEM((NW, 16, 128), BF16),
            DMA, DMA, DMA, DMA, DMA,
        ],
        compiler_params=pltpu.CompilerParams(vmem_limit_bytes=VMEM, has_side_effects=True),
    )(x, slots)


def transform(own, matrices, received, lat):
    cosine, logsin, weight, start = constants()
    pressure, depths, modes, project, heat = matrices
    return pl.pallas_call(
        transform_kernel,
        out_shape=(
            jax.ShapeDtypeStruct((NW, 16, 128), BF16),
            jax.ShapeDtypeStruct((2, SLOTS, 8, WAVES), BF16),
        ),
        in_specs=[smem()] * 7 + [vmem()] * 5,
        out_specs=(vmem(), vmem()),
        scratch_shapes=[
            pltpu.VMEM((8, PAD), F32),
            pltpu.SMEM((8, PAD), F32),
            pltpu.VMEM((3, CHAIN, HEMI), BF16),
            pltpu.VMEM((16 * 32, 128), F32),
            pltpu.VMEM((NW * 16, 128), F32),
            pltpu.VMEM((NLAT, 256), BF16),
            pltpu.VMEM((HEMI, 256), F32),
            pltpu.VMEM((PAD, 128), F32),
            pltpu.VMEM((128, PAD), F32),
            pltpu.VMEM((640, 1024), BF16),
            pltpu.VMEM((NW, 24 * 128), BF16),
            pltpu.VMEM((HEMI, 256), BF16),
            DMA,
        ],
        compiler_params=pltpu.CompilerParams(vmem_limit_bytes=VMEM),
    )(
        own, jnp.asarray(start), pressure, depths, modes, project, heat,
        received, lat, jnp.asarray(cosine), jnp.asarray(logsin), jnp.asarray(weight),
    )


def backward(blocks, state, slots):
    return pl.pallas_call(
        backward_kernel,
        out_shape=(
            jax.ShapeDtypeStruct((2 * SLOTS, 8, WAVES), BF16),
            jax.ShapeDtypeStruct((8, ROWS, WAVES), BF16),
        ),
        in_specs=[vmem(), vmem(), vmem()],
        out_specs=(vmem(), vmem()),
        scratch_shapes=[
            pltpu.VMEM((SLOTS * NW, WAVES), BF16),
            pltpu.VMEM((NW * 16, 128), F32),
            pltpu.VMEM((NW, 16, 128), BF16),
            pltpu.VMEM((SLOTS, 8, WAVES), BF16),
            pltpu.VMEM((8, ROWS, WAVES), BF16),
            pltpu.VMEM((8, ROWS, WAVES), BF16),
            DMA, DMA, DMA, DMA, DMA, DMA, DMA,
        ],
        compiler_params=pltpu.CompilerParams(vmem_limit_bytes=VMEM, has_side_effects=True),
    )(blocks, state, slots)


def body(
    fourier,
    lat_rows,
    wave_slots,
    pressure_balance_operator,
    depths,
    vertical_modes,
    mode_projection,
    heat_link_operator,
):
    wave, core = lax.axis_index("wave"), lax.axis_index("lev")
    slots = wave_slots.reshape(NW, 2 * SLOTS)
    lat = lat_rows.reshape(NW, ROWS)
    ten = lax.dynamic_slice_in_dim(wave_slots, wave * 2 * SLOTS, 2 * SLOTS)
    own = jnp.where(core == 0, ten[np.array(ORDER[0])], ten[np.array(ORDER[1])])
    matrices = (
        pressure_balance_operator, depths, vertical_modes, mode_projection, heat_link_operator,
    )
    received = forward(fourier.reshape(8, ROWS, WAVES), slots)
    blocks, state = transform(own, matrices, received, lat)
    spectral, grid = backward(blocks, state, slots)
    return (
        spectral.reshape(2 * SLOTS, 2, 2, 2, WAVES),
        grid.reshape(2, 2, 2, ROWS, WAVES),
    )


def solution(mesh):
    in_specs = (P(None, None, "lev", "wave", None), P(), P(), P(), P(), P(), P(), P())
    out_specs = (P("wave", None, None, "lev", None), P(None, None, "lev", "wave", None))
    return jax.shard_map(body, mesh=mesh, in_specs=in_specs, out_specs=out_specs, check_vma=False)
```

```python
import functools
import math

import jax
import jax.numpy as jnp
import numpy as np
from jax import lax
from jax.experimental import pallas as pl
from jax.experimental.pallas import tpu as pltpu
from jax.sharding import PartitionSpec as P

MESH = pl.DeviceIdType.MESH
F32 = jnp.float32
BF16 = jnp.bfloat16

WAVES = 1280
NLAT = 2560
HEMI = NLAT // 2
NW = 128
ROWS = NLAT // NW
SLOTS = 5
TILES = HEMI // 128
CHAIN = 1296
BLOCKS = CHAIN // 16
PAD = 1408
ORDER = ((0, 1, 2, 3, 4), (6, 7, 8, 9, 5))
EARLY = 14
VMEM = 60 * 1024 * 1024
STRIDE = 17


def constants():
    colat = np.pi * (np.arange(HEMI) + 0.5) / NLAT
    mixed = np.array(list(range(8)) + [8, 9] * 4)
    cosine = np.cos(colat).reshape(TILES, 128)[mixed].astype(np.float32)
    logsin = np.log(np.sin(colat)).reshape(TILES, 128)[mixed].astype(np.float32)
    weight = (math.sqrt(math.pi / NLAT) * np.sin(colat)).reshape(TILES, 128).T.astype(np.float32)
    start = np.array(
        [
            0.5 * (math.lgamma(m + 1.5) - math.lgamma(m + 1.0) - math.lgamma(1.5) - math.log(2.0))
            for m in range(WAVES)
        ],
        np.float32,
    )
    return cosine, logsin, weight, start


def iota(shape, axis):
    return lax.broadcasted_iota(jnp.int32, shape, axis)


def onehot(condition):
    return jnp.where(condition, 1.0, 0.0).astype(BF16)


def slot_onehot(core, slots_ref, hot):
    numbers = slots_ref[...]
    waves = iota((NW, WAVES), 1)
    for s in range(SLOTS):
        mine = jnp.where(
            core == 0,
            numbers[:, ORDER[0][s] : ORDER[0][s] + 1],
            numbers[:, ORDER[1][s] : ORDER[1][s] + 1],
        )
        hot[s * NW : (s + 1) * NW, :] = onehot(mine == waves)


def remote(src, dst, send_sem, recv_sem, device):
    return pltpu.make_async_remote_copy(
        src_ref=src, dst_ref=dst, send_sem=send_sem, recv_sem=recv_sem,
        device_id=device, device_id_type=MESH,
    )


def split(value):
    high = value.astype(BF16)
    return high, (value - high.astype(F32)).astype(BF16)


def product_of_parts(value, high, low):
    one, two = split(value)
    return jnp.dot(
        jnp.concatenate([one, two], axis=1),
        jnp.concatenate([high, high], axis=0),
        preferred_element_type=F32,
    ) + jnp.dot(one, low, preferred_element_type=F32)


def kernel(
    waves_ref, start_ref, pressure_ref, depths_ref, modes_ref, project_ref, heat_ref,
    x_ref, slots_ref, lat_ref, cosine_ref, logsin_ref, weight_ref,
    grid_mine_ref, grid_other_ref, state_mine_ref, state_other_ref,
    other, hot, rows, wide, send, land, send_back, land_back,
    coef_v, coef_s, table, block, folded_in, folds, spec, turned, shuffle, north_south,
    ns_rows, mirror_ref, sign_ref, small, state_half, state_land, left, half, half_land,
    round_two, coef_sem, pair_send, pair_recv, own_sem, send_sem, recv_sem,
    state_send, state_recv, own_back_sem, send_back_sem, recv_back_sem, half_send, half_recv,
):
    wave, core = lax.axis_index("wave"), lax.axis_index("lev")
    partner = (wave, 1 - core)
    lane = iota((1, 128), 1)

    depth_at, plane_at = lax.div(wave, 16), lax.rem(wave, 16)
    barrier = pltpu.get_barrier_semaphore()

    def greet_depth(i, _):
        there = lax.rem(depth_at + i, 8) * 16 + plane_at
        pl.semaphore_signal(barrier, inc=1, device_id=(there, core), device_id_type=MESH)
        return 0

    def in_plane(i):
        return depth_at * 16 + lax.rem(plane_at + i, 16)

    def greet_plane(i, _):
        pl.semaphore_signal(barrier, inc=1, device_id=(in_plane(i), core), device_id_type=MESH)
        return 0

    def pass_on(i, _):
        pl.semaphore_signal(round_two, inc=1, device_id=(in_plane(i), core), device_id_type=MESH)
        return 0

    pl.semaphore_signal(barrier, inc=1, device_id=partner, device_id_type=MESH)
    lax.fori_loop(1, 8, greet_depth, 0)
    lax.fori_loop(1, 16, greet_plane, 0)

    held = [
        jnp.where(
            core == 0,
            waves_ref[wave * 2 * SLOTS + ORDER[0][s]],
            waves_ref[wave * 2 * SLOTS + ORDER[1][s]],
        )
        for s in range(SLOTS)
    ]
    firsts = [held[0], held[2], held[4]]
    seconds = [held[1], held[3], 0]
    begins = [(WAVES - firsts[c] + 15) // 16 * 16 for c in range(2)] + [CHAIN + 16]

    j = iota((8, PAD), 1)
    row = iota((8, PAD), 0)

    def per_chain(values):
        which = row % 4
        return jnp.where(which == 0, values[0], jnp.where(which == 1, values[1], values[2]))

    begin = per_chain(begins)
    second = j >= begin
    order = jnp.where(second, per_chain(seconds), per_chain(firsts))
    k = jnp.where(second, j - begin, j)
    n = (order + k).astype(F32)
    m = order.astype(F32)
    ok = (k >= 1) & (order + k < WAVES)
    grow = jnp.sqrt((4.0 * n * n - 1.0) / jnp.where(ok, n * n - m * m, 1.0))
    less = n - 1.0
    damp = jnp.sqrt(
        jnp.where(ok, jnp.maximum(less * less - m * m, 0.0), 0.0)
        / jnp.where(ok & (less > 0.0), 4.0 * less * less - 1.0, 1.0)
    )
    coef = jnp.where(ok, jnp.where(row < 4, grow, grow * damp), 0.0)
    coef_v[...] = coef
    coef_copy = pltpu.make_async_copy(coef_v, coef_s, coef_sem)
    coef_copy.start()

    slot_onehot(core, slots_ref, hot)

    pl.semaphore_wait(barrier, 7 + 15 + 1)
    lax.fori_loop(1, 16, pass_on, 0)
    pair = remote(x_ref, other, pair_send, pair_recv, partner)
    pair.start()

    source = iota((1, 1024), 1)
    source = (source % 128) // 16 * 128 + source % 16 * 8 + source // 128
    valid = iota((1, 1024), 1) % 128 < 80
    shuffle[...] = onehot(valid & (iota((640, 1024), 0) == source))

    def place(ref, side):
        for f in range(8):
            value = ref[f].astype(F32)
            at = pl.multiple_of(side * 64 + f * 8, 8)
            rows[0, pl.ds(at, 8), :] = value[0:8]
            rows[1, pl.ds(at, 8), :] = value[8:16]
            rows[2, pl.ds(at, 8), :] = jnp.concatenate(
                [value[16:20], jnp.zeros((4, WAVES), F32)], axis=0
            )

    place(x_ref, core)

    cosine = [cosine_ref[0:8, :]] * 3 + [cosine_ref[8:16, :]]
    logsin = [logsin_ref[0:8, :]] * 3 + [logsin_ref[8:16, :]]
    sub = iota((8, 128), 0)

    def spread_rows(values):
        mixed = jnp.where(sub < 2, values[0], jnp.where(sub < 4, values[1], values[2]))
        return [values[0], values[1], values[2], mixed]

    def make(b, carry):
        current, former, scale = carry
        at_begin = [b * 16 == begins[c] for c in range(3)]
        wave_number = [
            jnp.where(at_begin[c], seconds[c], firsts[c]) for c in range(3)
        ]
        base = spread_rows([start_ref[w] for w in wave_number])
        degree = spread_rows([w.astype(F32) for w in wave_number])
        reset = spread_rows(
            [jnp.where((b == 0) | at_begin[c], 1.0, 0.0) for c in range(3)]
        )
        next_current, next_former, next_scale, factor = [], [], [], []
        for v in range(4):
            size = jnp.maximum(
                jnp.maximum(jnp.abs(current[v]), jnp.abs(former[v])), 1e-30
            )
            inverse = 1.0 / size
            again = reset[v] > 0.5
            if v < 3:
                again = jnp.broadcast_to(reset[v], (8, 128)) > 0.5
            next_current.append(jnp.where(again, 1.0, current[v] * inverse))
            next_former.append(jnp.where(again, 0.0, former[v] * inverse))
            next_scale.append(
                jnp.where(again, base[v] + degree[v] * logsin[v], scale[v] + jnp.log(size))
            )
            factor.append(jnp.exp(next_scale[v]))
        current, former = next_current, next_former
        for o in range(16):
            for v in range(4):
                block[pl.ds(v * 8 * STRIDE + o, 8, stride=STRIDE), :] = current[v] * factor[v]
            at = b * 16 + o + 1
            grow = spread_rows([coef_s[c, at] for c in range(3)])
            damp = spread_rows([coef_s[4 + c, at] for c in range(3)])
            following = [
                (cosine[v] * grow[v]) * current[v] - damp[v] * former[v] for v in range(4)
            ]
            former, current = current, following
        at = pl.multiple_of(b * 16, 16)
        for c in range(3):
            for t in range(TILES):
                line = c * 8 + t if t < 8 else 24 + 2 * c + t - 8
                table[c, pl.ds(at, 16), t * 128 : (t + 1) * 128] = block[
                    line * STRIDE : line * STRIDE + 16, :
                ].astype(BF16)
        return (tuple(current), tuple(former), tuple(next_scale))

    coef_copy.wait()
    zeros = tuple(jnp.zeros((8, 128), F32) for _ in range(4))
    carry = lax.fori_loop(0, EARLY, make, (zeros, zeros, zeros))

    pair.wait()
    place(other, 1 - core)
    wide[pl.ds(15, NW, stride=STRIDE), :] = jnp.zeros((NW, 128), F32)
    for c in range(3):
        arranged = lax.dot_general(
            hot[...], rows[c].astype(BF16), (((1,), (1,)), ((), ())), preferred_element_type=F32
        )
        for s in range(SLOTS):
            wide[pl.ds(c * 5 + s, NW, stride=STRIDE), :] = arranged[s * NW : (s + 1) * NW]
    for w in range(NW):
        send[w] = wide[w * STRIDE : w * STRIDE + 16, :].astype(BF16)
    pl.semaphore_wait(round_two, 15)
    own = pltpu.make_async_copy(send.at[wave], land.at[wave], own_sem)
    own.start()

    def send_to(step):
        target = lax.rem(wave + step, NW)
        remote(send.at[target], land.at[wave], send_sem, recv_sem, (target, core)).start()

    def make_and_send(i, carry):
        send_to(2 * i + 1)
        send_to(2 * i + 2)
        return make(EARLY + i, carry)

    carry = lax.fori_loop(0, NW // 2 - 1, make_and_send, carry)
    send_to(NW - 1)
    lax.fori_loop(EARLY + NW // 2 - 1, BLOCKS, make, carry)

    lat = lat_ref[...]
    sign = jnp.where(lat < HEMI, 1.0, -1.0)
    mirror = jnp.minimum(lat, NLAT - 1 - lat)
    mirror_rows = jnp.transpose(
        jnp.concatenate([mirror.astype(F32), jnp.zeros((NW, 128 - ROWS), F32)], axis=1)
    ).astype(jnp.int32)
    mirror_line = jnp.concatenate([mirror_rows[r : r + 1, :] for r in range(ROWS)], axis=1)

    mirror_ref[...] = mirror
    sign_ref[...] = sign

    own.wait()
    all_but_one = pl.ds(0, NW - 1)
    pltpu.make_async_copy(send.at[all_but_one], land.at[all_but_one], send_sem).wait()
    pltpu.make_async_copy(send.at[all_but_one], land.at[all_but_one], recv_sem).wait()

    for w in range(NW):
        wide[w * STRIDE : w * STRIDE + 16, :] = land[w].astype(F32)
    for c in range(3):
        piece = jnp.concatenate(
            [wide[pl.ds(c * 5 + s, NW, stride=STRIDE), :].astype(BF16) for s in range(SLOTS)],
            axis=1,
        )
        spread = jnp.dot(piece, shuffle[...], preferred_element_type=F32)
        for r in range(8 if c < 2 else 4):
            at = c * 8 + r
            part = spread[:, r * 128 : (r + 1) * 128]
            folded_in[at * NW : (at + 1) * NW, 0:128] = part.astype(BF16)
            folded_in[at * NW : (at + 1) * NW, 128:256] = (part * sign[:, at : at + 1]).astype(BF16)

    def fold(t, _):
        hot = onehot(mirror_line == iota((256, NLAT), 0) + t * 256)
        total = jnp.dot(hot, folded_in[...], preferred_element_type=F32)
        at = pl.multiple_of(t * 256, 256)
        folds[pl.ds(at, 256), :] = total
        return 0

    lax.fori_loop(0, HEMI // 256, fold, 0)
    for t in range(TILES):
        north_south[t * 128 : (t + 1) * 128, :] = (
            folds[t * 128 : (t + 1) * 128, :] * weight_ref[:, t : t + 1]
        ).astype(BF16)

    chain_of = lane // 32

    def lanes(values):
        return jnp.where(chain_of == 0, values[0], jnp.where(chain_of == 1, values[1], values[2]))

    is_second = (lane // 16) % 2 == 1
    lane_begin = lanes(begins)
    offset = jnp.where(is_second, lanes(seconds) - lane_begin, lanes(firsts))
    level = (lane // 8) % 2 * 2 + lane % 2
    field = (lane // 2) % 2
    depth = jnp.zeros((1, 128), F32)
    for a in range(4):
        depth = jnp.where(level == a, depths_ref[a], depth)
    across, down = iota((128, 128), 1), iota((128, 128), 0)
    same = (across // 16 == down // 16) & ((across // 4) % 2 == (down // 4) % 2)
    level_to, level_from = (across // 8) % 2 * 2 + across % 2, (down // 8) % 2 * 2 + down % 2
    field_to, field_from = (across // 2) % 2, (down // 2) % 2

    def matrix(entry, to, of):
        total = jnp.zeros((128, 128), F32)
        for a in range(4):
            for b in range(4):
                total = jnp.where((level_to == a) & (level_from == b), entry(a, b), total)
        return jnp.where(same & (field_to == to) & (field_from == of), total, 0.0)

    def product(one, two):
        return lambda a, b: sum(one[a, e] * two[e, b] for e in range(4))

    first_matrix = jnp.concatenate(
        [
            matrix(lambda a, b: project_ref[a, b], 0, 0),
            matrix(product(project_ref, pressure_ref), 0, 1),
        ],
        axis=1,
    )
    second_matrix = matrix(lambda a, b: modes_ref[a, b], 0, 0) - matrix(
        product(heat_ref, modes_ref), 1, 0
    )
    first_parts, second_parts = split(first_matrix), split(second_matrix)
    turned[:, CHAIN - 16 : PAD] = jnp.zeros((128, PAD - CHAIN + 16), F32)
    spec[CHAIN - 16 : PAD, :] = jnp.zeros((PAD - CHAIN + 16, 128), F32)
    step_rows = CHAIN // 3

    def solve(q, _):
        at = pl.multiple_of(q * step_rows, 16)
        j = iota((step_rows, 128), 0) + at
        parts = []
        for c in range(3):
            both = jnp.dot(
                table[c, pl.ds(at, step_rows), :], north_south[...], preferred_element_type=F32
            )
            parts.append(jnp.where(j % 2 == 0, both[:, 0:128], both[:, 128:256]))
        spectrum = jnp.where(chain_of == 0, parts[0], jnp.where(chain_of == 1, parts[1], parts[2]))
        spectrum = jnp.where((j >= lane_begin) == is_second, spectrum, 0.0)
        n = (j + offset).astype(F32)
        coupling = n * (n + 1.0) * (1.0 / float(WAVES * WAVES))
        mixed = product_of_parts(spectrum, *first_parts)
        scaled = (mixed[:, 0:128] + coupling * mixed[:, 128:256]) / (1.0 + coupling * depth)
        updated = product_of_parts(scaled, *second_parts) + jnp.where(field == 1, spectrum, 0.0)
        spec[pl.ds(at, step_rows), :] = updated.astype(BF16).astype(F32)
        return 0

    lax.fori_loop(0, 3, solve, 0)
    for t in range(PAD // 128):
        turned[:, t * 128 : (t + 1) * 128] = jnp.transpose(spec[t * 128 : (t + 1) * 128, :])
    for s in range(SLOTS):
        for v in range(2):
            value = turned[s * 16 + v * 8 : s * 16 + v * 8 + 8, :]
            if s % 2 == 1:
                for bit in range(4, 11):
                    moved = pltpu.roll(value, PAD - (1 << bit) % PAD, 1)
                    value = jnp.where((begins[s // 2] >> bit) % 2 == 1, moved, value)
            state_half[v, s] = value[:, 0:WAVES].astype(BF16)
    state_copy = remote(
        state_half.at[1 - core], state_land, state_send, state_recv, partner
    )
    state_copy.start()

    even = iota((1, CHAIN), 1) % 2 == 0
    inverse_scale = 1.0 / math.sqrt(WAVES)
    ns_rows[:, 96:128, :] = jnp.zeros((2, 32, HEMI), F32)
    for c in range(3):
        state = turned[c * 32 : c * 32 + 32, 0:CHAIN]
        both_parities = jnp.concatenate(
            [jnp.where(even, state, 0.0), jnp.where(even, 0.0, state)], axis=0
        ).astype(BF16)
        for t in range(HEMI // 256):
            both = jnp.dot(
                both_parities, table[c, :, t * 256 : (t + 1) * 256], preferred_element_type=F32
            )
            sym, anti = both[0:32], both[32:64]
            ns_rows[0, c * 32 : c * 32 + 32, t * 256 : (t + 1) * 256] = (sym + anti) * inverse_scale
            ns_rows[1, c * 32 : c * 32 + 32, t * 256 : (t + 1) * 256] = (sym - anti) * inverse_scale
    for u in range(2):
        for t in range(TILES):
            north_south[t * 128 : (t + 1) * 128, u * 128 : (u + 1) * 128] = jnp.transpose(
                ns_rows[u, :, t * 128 : (t + 1) * 128]
            ).astype(BF16)

    latitudes = iota((32, HEMI), 1)
    small[pl.ds(15, 32, stride=STRIDE), :] = jnp.zeros((32, 128), F32)
    own_back = pltpu.make_async_copy(send_back.at[wave], land_back.at[wave], own_back_sem)
    for g in range(4):
        base = pl.multiple_of(lax.rem(lax.div(wave, 32) + g, 4) * 32, 32)
        near = mirror_ref[pl.ds(base, 32), :]
        side = sign_ref[pl.ds(base, 32), :]
        hot_rows = jnp.concatenate(
            [onehot(near[:, r : r + 1] == latitudes) for r in range(ROWS)], axis=0
        )
        both = jnp.dot(hot_rows, north_south[...], preferred_element_type=F32)
        parts = [
            jnp.where(
                side[:, r : r + 1] > 0.0,
                both[r * 32 : (r + 1) * 32, 0:128],
                both[r * 32 : (r + 1) * 32, 128:256],
            ).astype(BF16)
            for r in range(ROWS)
        ] + [jnp.zeros((32, 128), BF16)] * 4
        line = jnp.concatenate(
            [jnp.concatenate(parts[c * 8 : c * 8 + 8], axis=1) for c in range(3)], axis=0
        )
        piece = lax.dot_general(
            line, shuffle[...], (((1,), (1,)), ((), ())), preferred_element_type=F32
        )
        for c in range(3):
            for s in range(SLOTS):
                small[pl.ds(c * 5 + s, 32, stride=STRIDE), :] = piece[
                    c * 32 : c * 32 + 32, s * 128 : (s + 1) * 128
                ]
        for w in range(32):
            send_back[base + w] = small[w * STRIDE : w * STRIDE + 16, :].astype(BF16)

        def give(i, _, base=base):
            target = base + lax.rem(wave + i, 32)
            remote(
                send_back.at[target], land_back.at[wave], send_back_sem, recv_back_sem,
                (target, core),
            ).start()
            return 0

        if g == 0:
            own_back.start()
        lax.fori_loop(1 if g == 0 else 0, 32, give, 0)

    state_copy.wait()
    for s in range(SLOTS):
        mine = jnp.where(core == 0, state_half[0, s].astype(F32), state_half[1, s].astype(F32))
        theirs = state_land[s].astype(F32)
        none = jnp.zeros_like(mine)
        state_mine_ref[ORDER[0][s]] = jnp.where(core == 0, mine, none).astype(BF16)
        state_mine_ref[ORDER[1][s]] = jnp.where(core == 0, none, mine).astype(BF16)
        state_other_ref[ORDER[0][s]] = jnp.where(core == 0, none, theirs).astype(BF16)
        state_other_ref[ORDER[1][s]] = jnp.where(core == 0, theirs, none).astype(BF16)
    own_back.wait()
    pltpu.make_async_copy(
        send_back.at[all_but_one], land_back.at[all_but_one], send_back_sem
    ).wait()
    pltpu.make_async_copy(
        send_back.at[all_but_one], land_back.at[all_but_one], recv_back_sem
    ).wait()

    for w in range(NW):
        wide[w * STRIDE : w * STRIDE + 16, :] = land_back[w].astype(F32)
    for c in range(3):
        for s in range(SLOTS):
            left[:, c, :, s * 128 : (s + 1) * 128] = (
                jnp.transpose(wide[pl.ds(c * 5 + s, NW, stride=STRIDE), :])
                .astype(BF16)
                .reshape(2, 64, 128)
            )

    def columns(side, ref):
        for c in range(3):
            value = jnp.dot(left[side, c], hot[...], preferred_element_type=F32).astype(BF16)
            for f in range(8):
                ref[f, c * 8 : min(c * 8 + 8, ROWS), :] = value[f * 8 : f * 8 + min(8, ROWS - c * 8)]

    columns(1 - core, half)
    half_copy = remote(half, half_land, half_send, half_recv, partner)
    half_copy.start()
    columns(core, grid_mine_ref)
    half_copy.wait()
    grid_other_ref[...] = half_land[...]


def vmem():
    return pl.BlockSpec(memory_space=pltpu.VMEM)


def smem():
    return pl.BlockSpec(memory_space=pltpu.SMEM)


def run(wave_slots, matrices, x, slots, lat):
    cosine, logsin, weight, start = constants()
    pressure, depths, modes, project, heat = matrices
    dma = pltpu.SemaphoreType.DMA
    return pl.pallas_call(
        kernel,
        out_shape=(
            jax.ShapeDtypeStruct((8, ROWS, WAVES), BF16),
            jax.ShapeDtypeStruct((8, ROWS, WAVES), BF16),
            jax.ShapeDtypeStruct((2 * SLOTS, 8, WAVES), BF16),
            jax.ShapeDtypeStruct((2 * SLOTS, 8, WAVES), BF16),
        ),
        in_specs=[smem()] * 7 + [vmem()] * 6,
        out_specs=(vmem(), vmem(), vmem(), vmem()),
        scratch_shapes=[
            pltpu.VMEM((8, ROWS, WAVES), BF16),
            pltpu.VMEM((SLOTS * NW, WAVES), BF16),
            pltpu.VMEM((3, 128, WAVES), F32),
            pltpu.VMEM((NW * STRIDE, 128), F32),
            pltpu.VMEM((NW, 16, 128), BF16),
            pltpu.VMEM((NW, 16, 128), BF16),
            pltpu.VMEM((NW, 16, 128), BF16),
            pltpu.VMEM((NW, 16, 128), BF16),
            pltpu.VMEM((8, PAD), F32),
            pltpu.SMEM((8, PAD), F32),
            pltpu.VMEM((3, CHAIN, HEMI), BF16),
            pltpu.VMEM((32 * STRIDE, 128), F32),
            pltpu.VMEM((NLAT, 256), BF16),
            pltpu.VMEM((HEMI, 256), F32),
            pltpu.VMEM((PAD, 128), F32),
            pltpu.VMEM((128, PAD), F32),
            pltpu.VMEM((640, 1024), BF16),
            pltpu.VMEM((HEMI, 256), BF16),
            pltpu.VMEM((2, 128, HEMI), F32),
            pltpu.VMEM((NW, ROWS), jnp.int32),
            pltpu.VMEM((NW, ROWS), F32),
            pltpu.VMEM((32 * STRIDE, 128), F32),
            pltpu.VMEM((2, SLOTS, 8, WAVES), BF16),
            pltpu.VMEM((SLOTS, 8, WAVES), BF16),
            pltpu.VMEM((2, 3, 64, 640), BF16),
            pltpu.VMEM((8, ROWS, WAVES), BF16),
            pltpu.VMEM((8, ROWS, WAVES), BF16),
            pltpu.SemaphoreType.REGULAR,
        ]
        + [dma] * 13,
        compiler_params=pltpu.CompilerParams(
            vmem_limit_bytes=VMEM, has_side_effects=True, collective_id=1
        ),
    )(
        wave_slots, jnp.asarray(start), pressure, depths, modes, project, heat,
        x, slots, lat, jnp.asarray(cosine), jnp.asarray(logsin), jnp.asarray(weight),
    )


def body(
    fourier,
    lat_rows,
    wave_slots,
    pressure_balance_operator,
    depths,
    vertical_modes,
    mode_projection,
    heat_link_operator,
):
    matrices = (
        pressure_balance_operator, depths, vertical_modes, mode_projection, heat_link_operator,
    )
    grid, grid_other, state, state_other = run(
        wave_slots,
        matrices,
        fourier.reshape(8, ROWS, WAVES),
        wave_slots.reshape(NW, 2 * SLOTS),
        lat_rows.reshape(NW, ROWS),
    )
    return (
        (state + state_other).reshape(2 * SLOTS, 2, 2, 2, WAVES),
        (grid + grid_other).reshape(2, 2, 2, ROWS, WAVES),
    )


def solution(mesh):
    in_specs = (P(None, None, "lev", "wave", None), P(), P(), P(), P(), P(), P(), P())
    out_specs = (P("wave", None, None, "lev", None), P(None, None, "lev", "wave", None))
    return jax.shard_map(body, mesh=mesh, in_specs=in_specs, out_specs=out_specs, check_vma=False)
```

```python
import functools
import math

import jax
import jax.numpy as jnp
import numpy as np
from jax import lax
from jax.experimental import pallas as pl
from jax.experimental.pallas import tpu as pltpu
from jax.sharding import PartitionSpec as P

MESH = pl.DeviceIdType.MESH
F32 = jnp.float32
BF16 = jnp.bfloat16

WAVES = 1280
NLAT = 2560
HEMI = NLAT // 2
NW = 128
ROWS = NLAT // NW
SLOTS = 5
PARTS = 21
KROWS = NW * 24
TILES = HEMI // 128
CHAIN = 1296
BLOCKS = CHAIN // 16
PAD = 1408
ORDER = ((0, 1, 2, 3, 4), (6, 7, 8, 9, 5))
EARLY = 14
VMEM = 60 * 1024 * 1024
STRIDE = 17


def constants():
    colat = np.pi * (np.arange(HEMI) + 0.5) / NLAT
    mixed = np.array(list(range(8)) + [8, 9] * 4)
    cosine = np.cos(colat).reshape(TILES, 128)[mixed].astype(np.float32)
    logsin = np.log(np.sin(colat)).reshape(TILES, 128)[mixed].astype(np.float32)
    weight = (math.sqrt(math.pi / NLAT) * np.sin(colat)).reshape(TILES, 128).T.astype(np.float32)
    start = np.array(
        [
            0.5 * (math.lgamma(m + 1.5) - math.lgamma(m + 1.0) - math.lgamma(1.5) - math.log(2.0))
            for m in range(WAVES)
        ],
        np.float32,
    )
    return cosine, logsin, weight, start


def iota(shape, axis):
    return lax.broadcasted_iota(jnp.int32, shape, axis)


def onehot(condition):
    return jnp.where(condition, 1.0, 0.0).astype(BF16)


def slot_onehot(core, slots_ref, hot):
    numbers = slots_ref[...]
    waves = iota((NW, WAVES), 1)
    for s in range(SLOTS):
        mine = jnp.where(
            core == 0,
            numbers[:, ORDER[0][s] : ORDER[0][s] + 1],
            numbers[:, ORDER[1][s] : ORDER[1][s] + 1],
        )
        hot[s * NW : (s + 1) * NW, :] = onehot(mine == waves)


def remote(src, dst, send_sem, recv_sem, device):
    return pltpu.make_async_remote_copy(
        src_ref=src, dst_ref=dst, send_sem=send_sem, recv_sem=recv_sem,
        device_id=device, device_id_type=MESH,
    )


def split(value):
    high = value.astype(BF16)
    return high, (value - high.astype(F32)).astype(BF16)


def product_of_parts(value, high, low):
    one, two = split(value)
    return jnp.dot(
        jnp.concatenate([one, two], axis=1),
        jnp.concatenate([high, high], axis=0),
        preferred_element_type=F32,
    ) + jnp.dot(one, low, preferred_element_type=F32)


def kernel(
    waves_ref, start_ref, pressure_ref, depths_ref, modes_ref, project_ref, heat_ref,
    x_ref, slots_ref, line_ref, cosine_ref, logsin_ref, weight_ref,
    grid_mine_ref, grid_other_ref, state_mine_ref, state_other_ref,
    other, hot, rows, wide, send, land, send_back, land_back,
    coef_v, coef_s, table, block, folded_in, folds, spec, turned, gathered, north_south,
    ns_rows, lat_rows, where, state_half, state_land, left, half, half_land,
    round_two, coef_sem, pair_send, pair_recv, own_sem, send_sem, recv_sem,
    state_send, state_recv, own_back_sem, send_back_sem, recv_back_sem, half_send, half_recv,
):
    wave, core = lax.axis_index("wave"), lax.axis_index("lev")
    partner = (wave, 1 - core)
    lane = iota((1, 128), 1)

    depth_at, plane_at = lax.div(wave, 16), lax.rem(wave, 16)
    barrier = pltpu.get_barrier_semaphore()

    def greet_depth(i, _):
        there = lax.rem(depth_at + i, 8) * 16 + plane_at
        pl.semaphore_signal(barrier, inc=1, device_id=(there, core), device_id_type=MESH)
        return 0

    def in_plane(i):
        return depth_at * 16 + lax.rem(plane_at + i, 16)

    def greet_plane(i, _):
        pl.semaphore_signal(barrier, inc=1, device_id=(in_plane(i), core), device_id_type=MESH)
        return 0

    def pass_on(i, _):
        pl.semaphore_signal(round_two, inc=1, device_id=(in_plane(i), core), device_id_type=MESH)
        return 0

    pl.semaphore_signal(barrier, inc=1, device_id=partner, device_id_type=MESH)
    lax.fori_loop(1, 8, greet_depth, 0)
    lax.fori_loop(1, 16, greet_plane, 0)

    held = [
        jnp.where(
            core == 0,
            waves_ref[wave * 2 * SLOTS + ORDER[0][s]],
            waves_ref[wave * 2 * SLOTS + ORDER[1][s]],
        )
        for s in range(SLOTS)
    ]
    firsts = [held[0], held[2], held[4]]
    seconds = [held[1], held[3], 0]
    begins = [(WAVES - firsts[c] + 15) // 16 * 16 for c in range(2)] + [CHAIN + 16]

    j = iota((8, PAD), 1)
    row = iota((8, PAD), 0)

    def per_chain(values):
        which = row % 4
        return jnp.where(which == 0, values[0], jnp.where(which == 1, values[1], values[2]))

    begin = per_chain(begins)
    second = j >= begin
    order = jnp.where(second, per_chain(seconds), per_chain(firsts))
    k = jnp.where(second, j - begin, j)
    n = (order + k).astype(F32)
    m = order.astype(F32)
    ok = (k >= 1) & (order + k < WAVES)
    grow = jnp.sqrt((4.0 * n * n - 1.0) / jnp.where(ok, n * n - m * m, 1.0))
    less = n - 1.0
    damp = jnp.sqrt(
        jnp.where(ok, jnp.maximum(less * less - m * m, 0.0), 0.0)
        / jnp.where(ok & (less > 0.0), 4.0 * less * less - 1.0, 1.0)
    )
    coef = jnp.where(ok, jnp.where(row < 4, grow, grow * damp), 0.0)
    coef_v[...] = coef
    coef_copy = pltpu.make_async_copy(coef_v, coef_s, coef_sem)
    coef_copy.start()

    slot_onehot(core, slots_ref, hot)

    pl.semaphore_wait(barrier, 7 + 15 + 1)
    lax.fori_loop(1, 16, pass_on, 0)
    pair = remote(x_ref, other, pair_send, pair_recv, partner)
    pair.start()

    def place(ref, side):
        for f in range(8):
            rows[side, f * PARTS : f * PARTS + ROWS, :] = ref[f].astype(F32)

    rows[...] = jnp.zeros((2, 8 * PARTS, WAVES), F32)
    place(x_ref, core)
    for q in range(KROWS // 128):
        lat_rows[q * 128 : (q + 1) * 128, :] = jnp.transpose(
            jnp.broadcast_to(line_ref[q : q + 1, :].astype(F32), (128, 128))
        )
    lat_line = jnp.concatenate([line_ref[q : q + 1, :] for q in range(KROWS // 128)], axis=1)
    mirror_line = jnp.minimum(lat_line, NLAT - 1 - lat_line)

    cosine = [cosine_ref[0:8, :]] * 3 + [cosine_ref[8:16, :]]
    logsin = [logsin_ref[0:8, :]] * 3 + [logsin_ref[8:16, :]]
    sub = iota((8, 128), 0)

    def spread_rows(values):
        mixed = jnp.where(sub < 2, values[0], jnp.where(sub < 4, values[1], values[2]))
        return [values[0], values[1], values[2], mixed]

    def make(b, carry):
        current, former, scale = carry
        at_begin = [b * 16 == begins[c] for c in range(3)]
        wave_number = [
            jnp.where(at_begin[c], seconds[c], firsts[c]) for c in range(3)
        ]
        base = spread_rows([start_ref[w] for w in wave_number])
        degree = spread_rows([w.astype(F32) for w in wave_number])
        reset = spread_rows(
            [jnp.where((b == 0) | at_begin[c], 1.0, 0.0) for c in range(3)]
        )
        next_current, next_former, next_scale, factor = [], [], [], []
        for v in range(4):
            size = jnp.maximum(
                jnp.maximum(jnp.abs(current[v]), jnp.abs(former[v])), 1e-30
            )
            inverse = 1.0 / size
            again = reset[v] > 0.5
            if v < 3:
                again = jnp.broadcast_to(reset[v], (8, 128)) > 0.5
            next_current.append(jnp.where(again, 1.0, current[v] * inverse))
            next_former.append(jnp.where(again, 0.0, former[v] * inverse))
            next_scale.append(
                jnp.where(again, base[v] + degree[v] * logsin[v], scale[v] + jnp.log(size))
            )
            factor.append(jnp.exp(next_scale[v]))
        current, former = next_current, next_former
        for o in range(16):
            for v in range(4):
                block[pl.ds(v * 8 * STRIDE + o, 8, stride=STRIDE), :] = current[v] * factor[v]
            at = b * 16 + o + 1
            grow = spread_rows([coef_s[c, at] for c in range(3)])
            damp = spread_rows([coef_s[4 + c, at] for c in range(3)])
            following = [
                (cosine[v] * grow[v]) * current[v] - damp[v] * former[v] for v in range(4)
            ]
            former, current = current, following
        at = pl.multiple_of(b * 16, 16)
        for c in range(3):
            for t in range(TILES):
                line = c * 8 + t if t < 8 else 24 + 2 * c + t - 8
                table[c, pl.ds(at, 16), t * 128 : (t + 1) * 128] = block[
                    line * STRIDE : line * STRIDE + 16, :
                ].astype(BF16)
        return (tuple(current), tuple(former), tuple(next_scale))

    coef_copy.wait()
    zeros = tuple(jnp.zeros((8, 128), F32) for _ in range(4))
    carry = lax.fori_loop(0, EARLY, make, (zeros, zeros, zeros))

    pair.wait()
    place(other, 1 - core)
    arranged = lax.dot_general(
        rows[...].reshape(16 * PARTS, WAVES).astype(BF16),
        hot[...],
        (((1,), (1,)), ((), ())),
        preferred_element_type=F32,
    )
    for s in range(SLOTS):
        gathered[s] = arranged[:, s * NW : (s + 1) * NW]
    ahead = lane < 80

    def one_row(r):
        return jnp.transpose(
            jnp.concatenate(
                [
                    gathered[s, pl.ds(r, 16, stride=PARTS), :]
                    for s in range(SLOTS)
                ]
                + [jnp.zeros((48, NW), F32)],
                axis=0,
            )
        )

    for r in range(4):
        last = one_row(16 + r)
        wide[pl.ds(r, NW, stride=STRIDE), :] = jnp.where(
            ahead, one_row(r), pltpu.roll(last, 80, 1)
        )
        wide[pl.ds(4 + r, NW, stride=STRIDE), :] = jnp.where(
            ahead, one_row(4 + r), pltpu.roll(last, 32, 1)
        )
    for r in range(8, 16):
        wide[pl.ds(r, NW, stride=STRIDE), :] = one_row(r)
    for w in range(NW):
        send[w] = wide[w * STRIDE : w * STRIDE + 16, :].astype(BF16)
    pl.semaphore_wait(round_two, 15)
    own = pltpu.make_async_copy(send.at[wave], land.at[wave], own_sem)
    own.start()

    def send_to(step, _):
        target = lax.rem(wave + step, NW)
        remote(send.at[target], land.at[wave], send_sem, recv_sem, (target, core)).start()
        return 0

    lax.fori_loop(1, NW, send_to, 0)
    lax.fori_loop(EARLY, BLOCKS, make, carry)

    def where_from(t, _):
        at = pl.multiple_of(t * 128, 128)
        where[pl.ds(at, 128), :] = onehot(mirror_line == iota((128, KROWS), 0) + t * 128)
        return 0

    lax.fori_loop(0, TILES, where_from, 0)

    own.wait()
    all_but_one = pl.ds(0, NW - 1)
    pltpu.make_async_copy(send.at[all_but_one], land.at[all_but_one], send_sem).wait()
    pltpu.make_async_copy(send.at[all_but_one], land.at[all_but_one], recv_sem).wait()

    received = land[...].astype(F32)
    sub = iota((NW, 8, 128), 1)
    lanes_of = iota((NW, 8, 128), 2)
    tops = received[:, 0:8, :].reshape(NW * 8, 128)
    three = pltpu.roll(tops, 48, 1).reshape(NW, 8, 128)
    two = pltpu.roll(tops, 96, 1).reshape(NW, 8, 128)
    late = jnp.where(
        sub < 4,
        jnp.where(lanes_of < 48, three, 0.0),
        jnp.where((lanes_of >= 48) & (lanes_of < 80), two, 0.0),
    ).reshape(NW * 8, 128)
    early = jnp.where(ahead, received.reshape(NW * 16, 128), 0.0)
    for at, part in ((0, early), (NW * 16, late)):
        end = at + part.shape[0]
        northern = lat_rows[at:end, :] < float(HEMI)
        folded_in[at:end, 0:128] = part.astype(BF16)
        folded_in[at:end, 128:256] = jnp.where(northern, part, -part).astype(BF16)

    def fold(t, _):
        at = pl.multiple_of(t * 256, 256)
        folds[pl.ds(at, 256), :] = jnp.dot(
            where[pl.ds(at, 256), :], folded_in[...], preferred_element_type=F32
        )
        return 0

    lax.fori_loop(0, HEMI // 256, fold, 0)
    for t in range(TILES):
        north_south[t * 128 : (t + 1) * 128, :] = (
            folds[t * 128 : (t + 1) * 128, :] * weight_ref[:, t : t + 1]
        ).astype(BF16)

    chain_of = lane // 32

    def lanes(values):
        return jnp.where(chain_of == 0, values[0], jnp.where(chain_of == 1, values[1], values[2]))

    is_second = (lane // 16) % 2 == 1
    lane_begin = lanes(begins)
    offset = jnp.where(is_second, lanes(seconds) - lane_begin, lanes(firsts))
    level = (lane // 8) % 2 * 2 + lane % 2
    field = (lane // 2) % 2
    depth = jnp.zeros((1, 128), F32)
    for a in range(4):
        depth = jnp.where(level == a, depths_ref[a], depth)
    across, down = iota((128, 128), 1), iota((128, 128), 0)
    same = (across // 16 == down // 16) & ((across // 4) % 2 == (down // 4) % 2)
    level_to, level_from = (across // 8) % 2 * 2 + across % 2, (down // 8) % 2 * 2 + down % 2
    field_to, field_from = (across // 2) % 2, (down // 2) % 2

    def matrix(entry, to, of):
        total = jnp.zeros((128, 128), F32)
        for a in range(4):
            for b in range(4):
                total = jnp.where((level_to == a) & (level_from == b), entry(a, b), total)
        return jnp.where(same & (field_to == to) & (field_from == of), total, 0.0)

    def product(one, two):
        return lambda a, b: sum(one[a, e] * two[e, b] for e in range(4))

    first_matrix = jnp.concatenate(
        [
            matrix(lambda a, b: project_ref[a, b], 0, 0),
            matrix(product(project_ref, pressure_ref), 0, 1),
        ],
        axis=1,
    )
    second_matrix = matrix(lambda a, b: modes_ref[a, b], 0, 0) - matrix(
        product(heat_ref, modes_ref), 1, 0
    )
    first_parts, second_parts = split(first_matrix), split(second_matrix)
    turned[:, CHAIN - 16 : PAD] = jnp.zeros((128, PAD - CHAIN + 16), F32)
    spec[CHAIN - 16 : PAD, :] = jnp.zeros((PAD - CHAIN + 16, 128), F32)
    step_rows = CHAIN // 3

    def solve(q, _):
        at = pl.multiple_of(q * step_rows, 16)
        j = iota((step_rows, 128), 0) + at
        parts = []
        for c in range(3):
            both = jnp.dot(
                table[c, pl.ds(at, step_rows), :], north_south[...], preferred_element_type=F32
            )
            parts.append(jnp.where(j % 2 == 0, both[:, 0:128], both[:, 128:256]))
        spectrum = jnp.where(chain_of == 0, parts[0], jnp.where(chain_of == 1, parts[1], parts[2]))
        spectrum = jnp.where((j >= lane_begin) == is_second, spectrum, 0.0)
        n = (j + offset).astype(F32)
        coupling = n * (n + 1.0) * (1.0 / float(WAVES * WAVES))
        mixed = product_of_parts(spectrum, *first_parts)
        scaled = (mixed[:, 0:128] + coupling * mixed[:, 128:256]) / (1.0 + coupling * depth)
        updated = product_of_parts(scaled, *second_parts) + jnp.where(field == 1, spectrum, 0.0)
        spec[pl.ds(at, step_rows), :] = updated.astype(BF16).astype(F32)
        return 0

    lax.fori_loop(0, 3, solve, 0)
    for t in range(PAD // 128):
        turned[:, t * 128 : (t + 1) * 128] = jnp.transpose(spec[t * 128 : (t + 1) * 128, :])
    for s in range(SLOTS):
        for v in range(2):
            value = turned[s * 16 + v * 8 : s * 16 + v * 8 + 8, :]
            if s % 2 == 1:
                for bit in range(4, 11):
                    moved = pltpu.roll(value, PAD - (1 << bit) % PAD, 1)
                    value = jnp.where((begins[s // 2] >> bit) % 2 == 1, moved, value)
            state_half[v, s] = value[:, 0:WAVES].astype(BF16)
    state_copy = remote(
        state_half.at[1 - core], state_land, state_send, state_recv, partner
    )
    state_copy.start()

    even = iota((1, CHAIN), 1) % 2 == 0
    inverse_scale = 1.0 / math.sqrt(WAVES)
    ns_rows[:, 96:128, :] = jnp.zeros((2, 32, HEMI), F32)
    for c in range(3):
        state = turned[c * 32 : c * 32 + 32, 0:CHAIN]
        both_parities = jnp.concatenate(
            [jnp.where(even, state, 0.0), jnp.where(even, 0.0, state)], axis=0
        ).astype(BF16)
        for t in range(HEMI // 256):
            both = jnp.dot(
                both_parities, table[c, :, t * 256 : (t + 1) * 256], preferred_element_type=F32
            )
            sym, anti = both[0:32], both[32:64]
            ns_rows[0, c * 32 : c * 32 + 32, t * 256 : (t + 1) * 256] = (sym + anti) * inverse_scale
            ns_rows[1, c * 32 : c * 32 + 32, t * 256 : (t + 1) * 256] = (sym - anti) * inverse_scale
    for u in range(2):
        for t in range(TILES):
            north_south[t * 128 : (t + 1) * 128, u * 128 : (u + 1) * 128] = jnp.transpose(
                ns_rows[u, :, t * 128 : (t + 1) * 128]
            ).astype(BF16)

    latitudes = iota((1, HEMI), 1).astype(F32)
    own_back = pltpu.make_async_copy(send_back.at[wave], land_back.at[wave], own_back_sem)
    sub = iota((32, 8, 128), 1)
    for g in range(4):
        base = pl.multiple_of(lax.rem(lax.div(wave, 32) + g, 4) * 32, 32)
        lat = jnp.concatenate(
            [
                lat_rows[pl.ds(pl.multiple_of(base * 16, 512), 512), :],
                lat_rows[pl.ds(pl.multiple_of(NW * 16 + base * 8, 256), 256), :],
            ],
            axis=0,
        )
        mirror = jnp.minimum(lat, float(NLAT - 1) - lat)
        hot_rows = jnp.concatenate(
            [
                onehot(mirror == latitudes[:, t * 128 : (t + 1) * 128])
                for t in range(TILES)
            ],
            axis=1,
        )
        both = jnp.dot(hot_rows, north_south[...], preferred_element_type=F32)
        part = jnp.where(lat < float(HEMI), both[:, 0:128], both[:, 128:256])
        late = part[512:768]
        late = jnp.where(
            sub < 4,
            pltpu.roll(late, 80, 1).reshape(32, 8, 128),
            pltpu.roll(late, 32, 1).reshape(32, 8, 128),
        )
        tile = part[0:512].reshape(32, 16, 128)
        send_back[pl.ds(base, 32)] = jnp.concatenate(
            [jnp.where(ahead.reshape(1, 1, 128), tile[:, 0:8], late), tile[:, 8:16]], axis=1
        ).astype(BF16)

        def give(i, _, base=base):
            target = base + lax.rem(wave + i, 32)
            remote(
                send_back.at[target], land_back.at[wave], send_back_sem, recv_back_sem,
                (target, core),
            ).start()
            return 0

        if g == 0:
            own_back.start()
        lax.fori_loop(1 if g == 0 else 0, 32, give, 0)

    state_copy.wait()
    for s in range(SLOTS):
        mine = jnp.where(core == 0, state_half[0, s].astype(F32), state_half[1, s].astype(F32))
        theirs = state_land[s].astype(F32)
        none = jnp.zeros_like(mine)
        state_mine_ref[ORDER[0][s]] = jnp.where(core == 0, mine, none).astype(BF16)
        state_mine_ref[ORDER[1][s]] = jnp.where(core == 0, none, mine).astype(BF16)
        state_other_ref[ORDER[0][s]] = jnp.where(core == 0, none, theirs).astype(BF16)
        state_other_ref[ORDER[1][s]] = jnp.where(core == 0, theirs, none).astype(BF16)
    own_back.wait()
    pltpu.make_async_copy(
        send_back.at[all_but_one], land_back.at[all_but_one], send_back_sem
    ).wait()
    pltpu.make_async_copy(
        send_back.at[all_but_one], land_back.at[all_but_one], recv_back_sem
    ).wait()

    for w in range(NW):
        wide[w * STRIDE : w * STRIDE + 16, :] = land_back[w].astype(F32)
    for r in range(16):
        value = jnp.transpose(wide[pl.ds(r, NW, stride=STRIDE), :])
        blocks = [(r, s) for s in range(SLOTS)]
        if r < 4:
            blocks += [(16 + r, s) for s in range(3)]
        elif r < 8:
            blocks += [(12 + r, s) for s in range(3, SLOTS)]
        for q, (at, s) in enumerate(blocks):
            for v in range(2):
                left[v, s, pl.ds(at, 8, stride=PARTS), :] = value[
                    q * 16 + v * 8 : q * 16 + v * 8 + 8
                ]

    def columns(side, ref):
        value = jnp.dot(
            jnp.concatenate([left[side, s].astype(BF16) for s in range(SLOTS)], axis=1),
            hot[...],
            preferred_element_type=F32,
        )
        for f in range(8):
            ref[f] = value[f * PARTS : f * PARTS + ROWS].astype(BF16)

    columns(1 - core, half)
    half_copy = remote(half, half_land, half_send, half_recv, partner)
    half_copy.start()
    columns(core, grid_mine_ref)
    half_copy.wait()
    grid_other_ref[...] = half_land[...]


def vmem():
    return pl.BlockSpec(memory_space=pltpu.VMEM)


def smem():
    return pl.BlockSpec(memory_space=pltpu.SMEM)


def run(wave_slots, matrices, x, slots, line):
    cosine, logsin, weight, start = constants()
    pressure, depths, modes, project, heat = matrices
    dma = pltpu.SemaphoreType.DMA
    return pl.pallas_call(
        kernel,
        out_shape=(
            jax.ShapeDtypeStruct((8, ROWS, WAVES), BF16),
            jax.ShapeDtypeStruct((8, ROWS, WAVES), BF16),
            jax.ShapeDtypeStruct((2 * SLOTS, 8, WAVES), BF16),
            jax.ShapeDtypeStruct((2 * SLOTS, 8, WAVES), BF16),
        ),
        in_specs=[smem()] * 7 + [vmem()] * 6,
        out_specs=(vmem(), vmem(), vmem(), vmem()),
        scratch_shapes=[
            pltpu.VMEM((8, ROWS, WAVES), BF16),
            pltpu.VMEM((SLOTS * NW, WAVES), BF16),
            pltpu.VMEM((2, 8 * PARTS, WAVES), F32),
            pltpu.VMEM((NW * STRIDE, 128), F32),
            pltpu.VMEM((NW, 16, 128), BF16),
            pltpu.VMEM((NW, 16, 128), BF16),
            pltpu.VMEM((NW, 16, 128), BF16),
            pltpu.VMEM((NW, 16, 128), BF16),
            pltpu.VMEM((8, PAD), F32),
            pltpu.SMEM((8, PAD), F32),
            pltpu.VMEM((3, CHAIN, HEMI), BF16),
            pltpu.VMEM((32 * STRIDE, 128), F32),
            pltpu.VMEM((KROWS, 256), BF16),
            pltpu.VMEM((HEMI, 256), F32),
            pltpu.VMEM((PAD, 128), F32),
            pltpu.VMEM((128, PAD), F32),
            pltpu.VMEM((SLOTS, 16 * PARTS, NW), F32),
            pltpu.VMEM((HEMI, 256), BF16),
            pltpu.VMEM((2, 128, HEMI), F32),
            pltpu.VMEM((KROWS, 128), F32),
            pltpu.VMEM((HEMI, KROWS), BF16),
            pltpu.VMEM((2, SLOTS, 8, WAVES), BF16),
            pltpu.VMEM((SLOTS, 8, WAVES), BF16),
            pltpu.VMEM((2, SLOTS, 8 * PARTS, NW), F32),
            pltpu.VMEM((8, ROWS, WAVES), BF16),
            pltpu.VMEM((8, ROWS, WAVES), BF16),
            pltpu.SemaphoreType.REGULAR,
        ]
        + [dma] * 13,
        compiler_params=pltpu.CompilerParams(
            vmem_limit_bytes=VMEM, has_side_effects=True, collective_id=1
        ),
    )(
        wave_slots, jnp.asarray(start), pressure, depths, modes, project, heat,
        x, slots, line, jnp.asarray(cosine), jnp.asarray(logsin), jnp.asarray(weight),
    )


def body(
    fourier,
    lat_rows,
    wave_slots,
    pressure_balance_operator,
    depths,
    vertical_modes,
    mode_projection,
    heat_link_operator,
):
    matrices = (
        pressure_balance_operator, depths, vertical_modes, mode_projection, heat_link_operator,
    )
    by_device = lat_rows.reshape(NW, ROWS)
    first = by_device[:, 0:16].reshape(NW * 16)
    last = jnp.concatenate([by_device[:, 16:20]] * 2, axis=1).reshape(NW * 8)
    grid, grid_other, state, state_other = run(
        wave_slots,
        matrices,
        fourier.reshape(8, ROWS, WAVES),
        wave_slots.reshape(NW, 2 * SLOTS),
        jnp.concatenate([first, last]).reshape(KROWS // 128, 128),
    )
    return (
        (state + state_other).reshape(2 * SLOTS, 2, 2, 2, WAVES),
        (grid + grid_other).reshape(2, 2, 2, ROWS, WAVES),
    )


def solution(mesh):
    in_specs = (P(None, None, "lev", "wave", None), P(), P(), P(), P(), P(), P(), P())
    out_specs = (P("wave", None, None, "lev", None), P(None, None, "lev", "wave", None))
    return jax.shard_map(body, mesh=mesh, in_specs=in_specs, out_specs=out_specs, check_vma=False)
```

```python
import functools
import math

import jax
import jax.numpy as jnp
import numpy as np
from jax import lax
from jax.experimental import pallas as pl
from jax.experimental.pallas import tpu as pltpu
from jax.sharding import PartitionSpec as P

MESH = pl.DeviceIdType.MESH
F32 = jnp.float32
BF16 = jnp.bfloat16

WAVES = 1280
NLAT = 2560
HEMI = NLAT // 2
NW = 128
ROWS = NLAT // NW
SLOTS = 5
PARTS = 21
KROWS = NW * 24
TILES = HEMI // 128
CHAIN = 1296
BLOCKS = CHAIN // 16
PAD = 1408
ORDER = ((0, 1, 2, 3, 4), (6, 7, 8, 9, 5))
EARLY = 14
VMEM = 54 * 1024 * 1024
STRIDE = 17


def constants():
    colat = np.pi * (np.arange(HEMI) + 0.5) / NLAT
    mixed = np.array(list(range(8)) + [8, 9] * 4)
    cosine = np.cos(colat).reshape(TILES, 128)[mixed].astype(np.float32)
    logsin = np.log(np.sin(colat)).reshape(TILES, 128)[mixed].astype(np.float32)
    weight = (math.sqrt(math.pi / NLAT) * np.sin(colat)).reshape(TILES, 128).T.astype(np.float32)
    start = np.array(
        [
            0.5 * (math.lgamma(m + 1.5) - math.lgamma(m + 1.0) - math.lgamma(1.5) - math.log(2.0))
            for m in range(WAVES)
        ],
        np.float32,
    )
    return cosine, logsin, weight, start


def iota(shape, axis):
    return lax.broadcasted_iota(jnp.int32, shape, axis)


def onehot(condition):
    return jnp.where(condition, 1.0, 0.0).astype(BF16)


def columns_of(line_ref, first, count, out):
    for q in range(count):
        out[q * 128 : (q + 1) * 128, :] = jnp.transpose(
            jnp.broadcast_to(line_ref[first + q : first + q + 1, :].astype(F32), (128, 128))
        )


def slot_onehot(core, numbers, hot):
    waves = iota((1, WAVES), 1).astype(F32)
    for s in range(SLOTS):
        mine = jnp.where(
            core == 0,
            numbers[pl.ds(ORDER[0][s], NW, stride=2 * SLOTS), :],
            numbers[pl.ds(ORDER[1][s], NW, stride=2 * SLOTS), :],
        )
        for t in range(TILES):
            hot[s * NW : (s + 1) * NW, t * 128 : (t + 1) * 128] = onehot(
                mine == waves[:, t * 128 : (t + 1) * 128]
            )


def remote(src, dst, send_sem, recv_sem, device):
    return pltpu.make_async_remote_copy(
        src_ref=src, dst_ref=dst, send_sem=send_sem, recv_sem=recv_sem,
        device_id=device, device_id_type=MESH,
    )


def split(value):
    high = value.astype(BF16)
    return high, (value - high.astype(F32)).astype(BF16)


def product_of_parts(value, high, low):
    one, two = split(value)
    return jnp.dot(
        jnp.concatenate([one, two], axis=1),
        jnp.concatenate([high, high], axis=0),
        preferred_element_type=F32,
    ) + jnp.dot(one, low, preferred_element_type=F32)


def kernel(
    waves_ref, start_ref, pressure_ref, depths_ref, modes_ref, project_ref, heat_ref,
    x_ref, line_ref, cosine_ref, logsin_ref, weight_ref,
    grid_mine_ref, grid_other_ref, state_mine_ref, state_other_ref,
    other, hot, rows, wide, send, land, send_back, land_back,
    coef_v, coef_s, table, block, folded_in, folds, spec, turned, gathered, north_south,
    ns_rows, numbers, lat_rows, lat_late, where, hot_rows, state_half, state_land, left, half, half_land,
    round_two, coef_sem, pair_send, pair_recv, own_sem, send_sem, recv_sem,
    state_send, state_recv, own_back_sem, send_back_sem, recv_back_sem, half_send, half_recv,
):
    wave, core = lax.axis_index("wave"), lax.axis_index("lev")
    partner = (wave, 1 - core)
    lane = iota((1, 128), 1)

    depth_at, plane_at = lax.div(wave, 16), lax.rem(wave, 16)
    barrier = pltpu.get_barrier_semaphore()

    def greet_depth(i, _):
        there = lax.rem(depth_at + i, 8) * 16 + plane_at
        pl.semaphore_signal(barrier, inc=1, device_id=(there, core), device_id_type=MESH)
        return 0

    def in_plane(i):
        return depth_at * 16 + lax.rem(plane_at + i, 16)

    def greet_plane(i, _):
        pl.semaphore_signal(barrier, inc=1, device_id=(in_plane(i), core), device_id_type=MESH)
        return 0

    def pass_on(i, _):
        pl.semaphore_signal(round_two, inc=1, device_id=(in_plane(i), core), device_id_type=MESH)
        return 0

    pl.semaphore_signal(barrier, inc=1, device_id=partner, device_id_type=MESH)
    lax.fori_loop(1, 8, greet_depth, 0)
    lax.fori_loop(1, 16, greet_plane, 0)

    held = [
        jnp.where(
            core == 0,
            waves_ref[wave * 2 * SLOTS + ORDER[0][s]],
            waves_ref[wave * 2 * SLOTS + ORDER[1][s]],
        )
        for s in range(SLOTS)
    ]
    firsts = [held[0], held[2], held[4]]
    seconds = [held[1], held[3], 0]
    begins = [(WAVES - firsts[c] + 15) // 16 * 16 for c in range(2)] + [CHAIN + 16]

    j = iota((8, PAD), 1)
    row = iota((8, PAD), 0)

    def per_chain(values):
        which = row % 4
        return jnp.where(which == 0, values[0], jnp.where(which == 1, values[1], values[2]))

    begin = per_chain(begins)
    second = j >= begin
    order = jnp.where(second, per_chain(seconds), per_chain(firsts))
    k = jnp.where(second, j - begin, j)
    n = (order + k).astype(F32)
    m = order.astype(F32)
    ok = (k >= 1) & (order + k < WAVES)
    grow = jnp.sqrt((4.0 * n * n - 1.0) / jnp.where(ok, n * n - m * m, 1.0))
    less = n - 1.0
    damp = jnp.sqrt(
        jnp.where(ok, jnp.maximum(less * less - m * m, 0.0), 0.0)
        / jnp.where(ok & (less > 0.0), 4.0 * less * less - 1.0, 1.0)
    )
    coef = jnp.where(ok, jnp.where(row < 4, grow, grow * damp), 0.0)
    coef_v[...] = coef
    coef_copy = pltpu.make_async_copy(coef_v, coef_s, coef_sem)
    coef_copy.start()

    columns_of(line_ref, 0, WAVES // 128, numbers)
    slot_onehot(core, numbers, hot)
    columns_of(line_ref, WAVES // 128, NLAT // 128, numbers)

    pl.semaphore_wait(barrier, 7 + 15 + 1)
    lax.fori_loop(1, 16, pass_on, 0)
    pair = remote(x_ref, other, pair_send, pair_recv, partner)
    pair.start()

    def place(ref, side):
        for f in range(8):
            rows[side, f * PARTS : f * PARTS + ROWS, :] = ref[f].astype(F32)

    rows[...] = jnp.zeros((2, 8 * PARTS, WAVES), F32)
    place(x_ref, core)
    for w in range(NW):
        last = numbers[w * ROWS + 16 : w * ROWS + 20, :]
        lat_rows[w // 4, w % 4] = numbers[w * ROWS : w * ROWS + 16, :]
        lat_late[w // 4, w % 4] = jnp.concatenate([last, last], axis=0)
    lat_line = jnp.concatenate(
        [
            jnp.transpose(lat_rows[q * 2 : q * 2 + 2].reshape(128, 128))[0:1, :]
            for q in range(NW // 8)
        ]
        + [
            jnp.transpose(lat_late[q * 4 : q * 4 + 4].reshape(128, 128))[0:1, :]
            for q in range(NW // 16)
        ],
        axis=1,
    ).astype(jnp.int32)
    mirror_line = jnp.minimum(lat_line, NLAT - 1 - lat_line)

    cosine = [cosine_ref[0:8, :]] * 3 + [cosine_ref[8:16, :]]
    logsin = [logsin_ref[0:8, :]] * 3 + [logsin_ref[8:16, :]]
    sub = iota((8, 128), 0)

    def spread_rows(values):
        mixed = jnp.where(sub < 2, values[0], jnp.where(sub < 4, values[1], values[2]))
        return [values[0], values[1], values[2], mixed]

    def make(b, carry):
        current, former, scale = carry
        at_begin = [b * 16 == begins[c] for c in range(3)]
        wave_number = [
            jnp.where(at_begin[c], seconds[c], firsts[c]) for c in range(3)
        ]
        base = spread_rows([start_ref[w] for w in wave_number])
        degree = spread_rows([w.astype(F32) for w in wave_number])
        reset = spread_rows(
            [jnp.where((b == 0) | at_begin[c], 1.0, 0.0) for c in range(3)]
        )
        next_current, next_former, next_scale, factor = [], [], [], []
        for v in range(4):
            size = jnp.maximum(
                jnp.maximum(jnp.abs(current[v]), jnp.abs(former[v])), 1e-30
            )
            inverse = 1.0 / size
            again = reset[v] > 0.5
            if v < 3:
                again = jnp.broadcast_to(reset[v], (8, 128)) > 0.5
            next_current.append(jnp.where(again, 1.0, current[v] * inverse))
            next_former.append(jnp.where(again, 0.0, former[v] * inverse))
            next_scale.append(
                jnp.where(again, base[v] + degree[v] * logsin[v], scale[v] + jnp.log(size))
            )
            factor.append(jnp.exp(next_scale[v]))
        current, former = next_current, next_former
        for o in range(16):
            for v in range(4):
                block[pl.ds(v * 8 * STRIDE + o, 8, stride=STRIDE), :] = current[v] * factor[v]
            at = b * 16 + o + 1
            grow = spread_rows([coef_s[c, at] for c in range(3)])
            damp = spread_rows([coef_s[4 + c, at] for c in range(3)])
            following = [
                (cosine[v] * grow[v]) * current[v] - damp[v] * former[v] for v in range(4)
            ]
            former, current = current, following
        at = pl.multiple_of(b * 16, 16)
        for c in range(3):
            for t in range(TILES):
                line = c * 8 + t if t < 8 else 24 + 2 * c + t - 8
                table[c, pl.ds(at, 16), t * 128 : (t + 1) * 128] = block[
                    line * STRIDE : line * STRIDE + 16, :
                ].astype(BF16)
        return (tuple(current), tuple(former), tuple(next_scale))

    coef_copy.wait()
    zeros = tuple(jnp.zeros((8, 128), F32) for _ in range(4))
    carry = lax.fori_loop(0, EARLY, make, (zeros, zeros, zeros))

    pair.wait()
    place(other, 1 - core)
    arranged = lax.dot_general(
        rows[...].reshape(16 * PARTS, WAVES).astype(BF16),
        hot[...],
        (((1,), (1,)), ((), ())),
        preferred_element_type=F32,
    )
    for s in range(SLOTS):
        gathered[s] = arranged[:, s * NW : (s + 1) * NW]
    ahead = lane < 80

    def one_row(r):
        return jnp.transpose(
            jnp.concatenate(
                [
                    gathered[s, pl.ds(r, 16, stride=PARTS), :]
                    for s in range(SLOTS)
                ]
                + [jnp.zeros((48, NW), F32)],
                axis=0,
            )
        )

    for r in range(4):
        last = one_row(16 + r)
        wide[pl.ds(r, NW, stride=STRIDE), :] = jnp.where(
            ahead, one_row(r), pltpu.roll(last, 80, 1)
        )
        wide[pl.ds(4 + r, NW, stride=STRIDE), :] = jnp.where(
            ahead, one_row(4 + r), pltpu.roll(last, 32, 1)
        )
    for r in range(8, 16):
        wide[pl.ds(r, NW, stride=STRIDE), :] = one_row(r)
    for w in range(NW):
        send[w] = wide[w * STRIDE : w * STRIDE + 16, :].astype(BF16)
    pl.semaphore_wait(round_two, 15)
    own = pltpu.make_async_copy(send.at[wave], land.at[wave], own_sem)
    own.start()

    def send_to(step, _):
        offset = lax.rem(step, 8) * 16 + lax.div(step, 8)
        target = lax.rem(wave + offset, NW)
        remote(send.at[target], land.at[wave], send_sem, recv_sem, (target, core)).start()
        return 0

    lax.fori_loop(1, NW, send_to, 0)
    lax.fori_loop(EARLY, BLOCKS, make, carry)

    def where_from(t, _):
        at = pl.multiple_of(t * 128, 128)
        where[pl.ds(at, 128), :] = onehot(mirror_line == iota((128, KROWS), 0) + t * 128)
        return 0

    lax.fori_loop(0, TILES, where_from, 0)

    latitudes = iota((1, HEMI), 1).astype(F32)

    def lats_at(x):
        return jnp.concatenate(
            [lat_rows[:, x].reshape(512, 128), lat_late[:, x].reshape(256, 128)], axis=0
        )

    def where_to(x, _):
        lat = lats_at(x)
        mirror = jnp.minimum(lat, float(NLAT - 1) - lat)
        for t in range(TILES):
            hot_rows[x, :, t * 128 : (t + 1) * 128] = onehot(
                mirror == latitudes[:, t * 128 : (t + 1) * 128]
            )
        return 0

    lax.fori_loop(0, 4, where_to, 0)

    chain_of = lane // 32

    def lanes(values):
        return jnp.where(chain_of == 0, values[0], jnp.where(chain_of == 1, values[1], values[2]))

    is_second = (lane // 16) % 2 == 1
    lane_begin = lanes(begins)
    offset = jnp.where(is_second, lanes(seconds) - lane_begin, lanes(firsts))
    level = (lane // 8) % 2 * 2 + lane % 2
    field = (lane // 2) % 2
    depth = jnp.zeros((1, 128), F32)
    for a in range(4):
        depth = jnp.where(level == a, depths_ref[a], depth)
    across, down = iota((128, 128), 1), iota((128, 128), 0)
    same = (across // 16 == down // 16) & ((across // 4) % 2 == (down // 4) % 2)
    level_to, level_from = (across // 8) % 2 * 2 + across % 2, (down // 8) % 2 * 2 + down % 2
    field_to, field_from = (across // 2) % 2, (down // 2) % 2

    def matrix(entry, to, of):
        total = jnp.zeros((128, 128), F32)
        for a in range(4):
            for b in range(4):
                total = jnp.where((level_to == a) & (level_from == b), entry(a, b), total)
        return jnp.where(same & (field_to == to) & (field_from == of), total, 0.0)

    def product(one, two):
        return lambda a, b: sum(one[a, e] * two[e, b] for e in range(4))

    first_matrix = jnp.concatenate(
        [
            matrix(lambda a, b: project_ref[a, b], 0, 0),
            matrix(product(project_ref, pressure_ref), 0, 1),
        ],
        axis=1,
    )
    second_matrix = matrix(lambda a, b: modes_ref[a, b], 0, 0) - matrix(
        product(heat_ref, modes_ref), 1, 0
    )
    first_parts, second_parts = split(first_matrix), split(second_matrix)
    turned[:, CHAIN - 16 : PAD] = jnp.zeros((128, PAD - CHAIN + 16), F32)
    spec[CHAIN - 16 : PAD, :] = jnp.zeros((PAD - CHAIN + 16, 128), F32)
    ns_rows[:, 96:128, :] = jnp.zeros((2, 32, HEMI), F32)

    own.wait()
    all_but_one = pl.ds(0, NW - 1)
    pltpu.make_async_copy(send.at[all_but_one], land.at[all_but_one], send_sem).wait()
    pltpu.make_async_copy(send.at[all_but_one], land.at[all_but_one], recv_sem).wait()

    received = land[...].astype(F32)
    sub = iota((NW, 8, 128), 1)
    lanes_of = iota((NW, 8, 128), 2)
    tops = received[:, 0:8, :].reshape(NW * 8, 128)
    three = pltpu.roll(tops, 48, 1).reshape(NW, 8, 128)
    two = pltpu.roll(tops, 96, 1).reshape(NW, 8, 128)
    late = jnp.where(
        sub < 4,
        jnp.where(lanes_of < 48, three, 0.0),
        jnp.where((lanes_of >= 48) & (lanes_of < 80), two, 0.0),
    ).reshape(NW * 8, 128)
    early = jnp.where(ahead, received.reshape(NW * 16, 128), 0.0)
    for at, part, lats in ((0, early, lat_rows), (NW * 16, late, lat_late)):
        end = at + part.shape[0]
        northern = lats[...].reshape(part.shape) < float(HEMI)
        folded_in[at:end, 0:128] = part.astype(BF16)
        folded_in[at:end, 128:256] = jnp.where(northern, part, -part).astype(BF16)

    def fold(t, _):
        at = pl.multiple_of(t * 256, 256)
        folds[pl.ds(at, 256), :] = jnp.dot(
            where[pl.ds(at, 256), :], folded_in[...], preferred_element_type=F32
        )
        return 0

    lax.fori_loop(0, HEMI // 256, fold, 0)
    for t in range(TILES):
        north_south[t * 128 : (t + 1) * 128, :] = (
            folds[t * 128 : (t + 1) * 128, :] * weight_ref[:, t : t + 1]
        ).astype(BF16)

    step_rows = CHAIN // 3

    def solve(q, _):
        at = pl.multiple_of(q * step_rows, 16)
        j = iota((step_rows, 128), 0) + at
        parts = []
        for c in range(3):
            both = jnp.dot(
                table[c, pl.ds(at, step_rows), :], north_south[...], preferred_element_type=F32
            )
            parts.append(jnp.where(j % 2 == 0, both[:, 0:128], both[:, 128:256]))
        spectrum = jnp.where(chain_of == 0, parts[0], jnp.where(chain_of == 1, parts[1], parts[2]))
        spectrum = jnp.where((j >= lane_begin) == is_second, spectrum, 0.0)
        n = (j + offset).astype(F32)
        coupling = n * (n + 1.0) * (1.0 / float(WAVES * WAVES))
        mixed = product_of_parts(spectrum, *first_parts)
        scaled = (mixed[:, 0:128] + coupling * mixed[:, 128:256]) / (1.0 + coupling * depth)
        updated = product_of_parts(scaled, *second_parts) + jnp.where(field == 1, spectrum, 0.0)
        spec[pl.ds(at, step_rows), :] = updated.astype(BF16).astype(F32)
        return 0

    lax.fori_loop(0, 3, solve, 0)
    for t in range(PAD // 128):
        turned[:, t * 128 : (t + 1) * 128] = jnp.transpose(spec[t * 128 : (t + 1) * 128, :])
    for s in range(SLOTS):
        for v in range(2):
            value = turned[s * 16 + v * 8 : s * 16 + v * 8 + 8, :]
            if s % 2 == 1:
                for bit in range(4, 11):
                    moved = pltpu.roll(value, PAD - (1 << bit) % PAD, 1)
                    value = jnp.where((begins[s // 2] >> bit) % 2 == 1, moved, value)
            state_half[v, s] = value[:, 0:WAVES].astype(BF16)
    state_copy = remote(
        state_half.at[1 - core], state_land, state_send, state_recv, partner
    )
    state_copy.start()

    even = iota((1, CHAIN), 1) % 2 == 0
    inverse_scale = 1.0 / math.sqrt(WAVES)
    for c in range(3):
        state = turned[c * 32 : c * 32 + 32, 0:CHAIN]
        both_parities = jnp.concatenate(
            [jnp.where(even, state, 0.0), jnp.where(even, 0.0, state)], axis=0
        ).astype(BF16)
        for t in range(HEMI // 256):
            both = jnp.dot(
                both_parities, table[c, :, t * 256 : (t + 1) * 256], preferred_element_type=F32
            )
            sym, anti = both[0:32], both[32:64]
            ns_rows[0, c * 32 : c * 32 + 32, t * 256 : (t + 1) * 256] = (sym + anti) * inverse_scale
            ns_rows[1, c * 32 : c * 32 + 32, t * 256 : (t + 1) * 256] = (sym - anti) * inverse_scale
    for u in range(2):
        for t in range(TILES):
            north_south[t * 128 : (t + 1) * 128, u * 128 : (u + 1) * 128] = jnp.transpose(
                ns_rows[u, :, t * 128 : (t + 1) * 128]
            ).astype(BF16)

    own_back = pltpu.make_async_copy(send_back.at[wave], land_back.at[wave], own_back_sem)
    sub = iota((32, 8, 128), 1)
    for g in range(4):
        x = lax.rem(wave + g, 4)
        lat = lats_at(x)
        both = jnp.dot(hot_rows[x], north_south[...], preferred_element_type=F32)
        part = jnp.where(lat < float(HEMI), both[:, 0:128], both[:, 128:256])
        late = part[512:768]
        late = jnp.where(
            sub < 4,
            pltpu.roll(late, 80, 1).reshape(32, 8, 128),
            pltpu.roll(late, 32, 1).reshape(32, 8, 128),
        )
        tile = part[0:512].reshape(32, 16, 128)
        tile = jnp.concatenate(
            [jnp.where(ahead.reshape(1, 1, 128), tile[:, 0:8], late), tile[:, 8:16]], axis=1
        ).astype(BF16)
        for i in range(32):
            send_back[i * 4 + x] = tile[i]

        def give(i, _, x=x):
            offset = lax.rem(i, 8) * 4 + lax.div(i, 8)
            target = lax.rem(lax.div(wave, 4) + offset, 32) * 4 + x
            remote(
                send_back.at[target], land_back.at[wave], send_back_sem, recv_back_sem,
                (target, core),
            ).start()
            return 0

        if g == 0:
            own_back.start()
        lax.fori_loop(1 if g == 0 else 0, 32, give, 0)

    state_copy.wait()
    for s in range(SLOTS):
        mine = jnp.where(core == 0, state_half[0, s].astype(F32), state_half[1, s].astype(F32))
        theirs = state_land[s].astype(F32)
        none = jnp.zeros_like(mine)
        state_mine_ref[ORDER[0][s]] = jnp.where(core == 0, mine, none).astype(BF16)
        state_mine_ref[ORDER[1][s]] = jnp.where(core == 0, none, mine).astype(BF16)
        state_other_ref[ORDER[0][s]] = jnp.where(core == 0, none, theirs).astype(BF16)
        state_other_ref[ORDER[1][s]] = jnp.where(core == 0, theirs, none).astype(BF16)
    own_back.wait()
    pltpu.make_async_copy(
        send_back.at[all_but_one], land_back.at[all_but_one], send_back_sem
    ).wait()
    pltpu.make_async_copy(
        send_back.at[all_but_one], land_back.at[all_but_one], recv_back_sem
    ).wait()

    for w in range(NW):
        wide[w * STRIDE : w * STRIDE + 16, :] = land_back[w].astype(F32)
    for r in range(16):
        value = jnp.transpose(wide[pl.ds(r, NW, stride=STRIDE), :])
        blocks = [(r, s) for s in range(SLOTS)]
        if r < 4:
            blocks += [(16 + r, s) for s in range(3)]
        elif r < 8:
            blocks += [(12 + r, s) for s in range(3, SLOTS)]
        for q, (at, s) in enumerate(blocks):
            for v in range(2):
                left[v, s, pl.ds(at, 8, stride=PARTS), :] = value[
                    q * 16 + v * 8 : q * 16 + v * 8 + 8
                ]

    def columns(side, ref):
        value = jnp.dot(
            jnp.concatenate([left[side, s].astype(BF16) for s in range(SLOTS)], axis=1),
            hot[...],
            preferred_element_type=F32,
        )
        for f in range(8):
            ref[f] = value[f * PARTS : f * PARTS + ROWS].astype(BF16)

    columns(1 - core, half)
    half_copy = remote(half, half_land, half_send, half_recv, partner)
    half_copy.start()
    columns(core, grid_mine_ref)
    half_copy.wait()
    grid_other_ref[...] = half_land[...]


def vmem():
    return pl.BlockSpec(memory_space=pltpu.VMEM)


def smem():
    return pl.BlockSpec(memory_space=pltpu.SMEM)


def run(wave_slots, matrices, x, line):
    cosine, logsin, weight, start = constants()
    pressure, depths, modes, project, heat = matrices
    dma = pltpu.SemaphoreType.DMA
    return pl.pallas_call(
        kernel,
        out_shape=(
            jax.ShapeDtypeStruct((8, ROWS, WAVES), BF16),
            jax.ShapeDtypeStruct((8, ROWS, WAVES), BF16),
            jax.ShapeDtypeStruct((2 * SLOTS, 8, WAVES), BF16),
            jax.ShapeDtypeStruct((2 * SLOTS, 8, WAVES), BF16),
        ),
        in_specs=[smem()] * 7 + [vmem()] * 5,
        out_specs=(vmem(), vmem(), vmem(), vmem()),
        scratch_shapes=[
            pltpu.VMEM((8, ROWS, WAVES), BF16),
            pltpu.VMEM((SLOTS * NW, WAVES), BF16),
            pltpu.VMEM((2, 8 * PARTS, WAVES), F32),
            pltpu.VMEM((NW * STRIDE, 128), F32),
            pltpu.VMEM((NW, 16, 128), BF16),
            pltpu.VMEM((NW, 16, 128), BF16),
            pltpu.VMEM((NW, 16, 128), BF16),
            pltpu.VMEM((NW, 16, 128), BF16),
            pltpu.VMEM((8, PAD), F32),
            pltpu.SMEM((8, PAD), F32),
            pltpu.VMEM((3, CHAIN, HEMI), BF16),
            pltpu.VMEM((32 * STRIDE, 128), F32),
            pltpu.VMEM((KROWS, 256), BF16),
            pltpu.VMEM((HEMI, 256), F32),
            pltpu.VMEM((PAD, 128), F32),
            pltpu.VMEM((128, PAD), F32),
            pltpu.VMEM((SLOTS, 16 * PARTS, NW), F32),
            pltpu.VMEM((HEMI, 256), BF16),
            pltpu.VMEM((2, 128, HEMI), F32),
            pltpu.VMEM((NLAT, 128), F32),
            pltpu.VMEM((32, 4, 16, 128), F32),
            pltpu.VMEM((32, 4, 8, 128), F32),
            pltpu.VMEM((HEMI, KROWS), BF16),
            pltpu.VMEM((4, KROWS // 4, HEMI), BF16),
            pltpu.VMEM((2, SLOTS, 8, WAVES), BF16),
            pltpu.VMEM((SLOTS, 8, WAVES), BF16),
            pltpu.VMEM((2, SLOTS, 8 * PARTS, NW), F32),
            pltpu.VMEM((8, ROWS, WAVES), BF16),
            pltpu.VMEM((8, ROWS, WAVES), BF16),
            pltpu.SemaphoreType.REGULAR,
        ]
        + [dma] * 13,
        compiler_params=pltpu.CompilerParams(
            vmem_limit_bytes=VMEM, has_side_effects=True, collective_id=1
        ),
    )(
        wave_slots, jnp.asarray(start), pressure, depths, modes, project, heat,
        x, line, jnp.asarray(cosine), jnp.asarray(logsin), jnp.asarray(weight),
    )


def body(
    fourier,
    lat_rows,
    wave_slots,
    pressure_balance_operator,
    depths,
    vertical_modes,
    mode_projection,
    heat_link_operator,
):
    matrices = (
        pressure_balance_operator, depths, vertical_modes, mode_projection, heat_link_operator,
    )
    grid, grid_other, state, state_other = run(
        wave_slots,
        matrices,
        fourier.reshape(8, ROWS, WAVES),
        jnp.concatenate([wave_slots, lat_rows]).reshape((WAVES + NLAT) // 128, 128),
    )
    return (
        (state + state_other).reshape(2 * SLOTS, 2, 2, 2, WAVES),
        (grid + grid_other).reshape(2, 2, 2, ROWS, WAVES),
    )


def solution(mesh):
    in_specs = (P(None, None, "lev", "wave", None), P(), P(), P(), P(), P(), P(), P())
    out_specs = (P("wave", None, None, "lev", None), P(None, None, "lev", "wave", None))
    return jax.shard_map(body, mesh=mesh, in_specs=in_specs, out_specs=out_specs, check_vma=False)
```

```python
import functools
import math

import jax
import jax.numpy as jnp
import numpy as np
from jax import lax
from jax.experimental import pallas as pl
from jax.experimental.pallas import tpu as pltpu
from jax.sharding import PartitionSpec as P

MESH = pl.DeviceIdType.MESH
F32 = jnp.float32
BF16 = jnp.bfloat16

WAVES = 1280
NLAT = 2560
HEMI = NLAT // 2
NW = 128
ROWS = NLAT // NW
SLOTS = 5
PARTS = 21
KROWS = NW * 24
TILES = HEMI // 128
CHAIN = 1296
BLOCKS = CHAIN // 16
PAD = 1408
ORDER = ((0, 1, 2, 3, 4), (6, 7, 8, 9, 5))
EARLY = 14
VMEM = 54 * 1024 * 1024
STRIDE = 17


def constants():
    colat = np.pi * (np.arange(HEMI) + 0.5) / NLAT
    mixed = np.array(list(range(8)) + [8, 9] * 4)
    cosine = np.cos(colat).reshape(TILES, 128)[mixed].astype(np.float32)
    logsin = np.log(np.sin(colat)).reshape(TILES, 128)[mixed].astype(np.float32)
    weight = (math.sqrt(math.pi / NLAT) * np.sin(colat)).reshape(TILES, 128).T.astype(np.float32)
    start = np.array(
        [
            0.5 * (math.lgamma(m + 1.5) - math.lgamma(m + 1.0) - math.lgamma(1.5) - math.log(2.0))
            for m in range(WAVES)
        ],
        np.float32,
    )
    return cosine, logsin, weight, start


def iota(shape, axis):
    return lax.broadcasted_iota(jnp.int32, shape, axis)


def onehot(condition):
    return jnp.where(condition, 1.0, 0.0).astype(BF16)


def columns_of(line_ref, count, out):
    for q in range(count):
        out[q * 128 : (q + 1) * 128, :] = jnp.transpose(
            jnp.broadcast_to(line_ref[q : q + 1, :].astype(F32), (128, 128))
        )


def slot_onehot(core, numbers, hot):
    waves = iota((1, WAVES), 1).astype(F32)
    for s in range(SLOTS):
        mine = jnp.where(
            core == 0,
            numbers[pl.ds(ORDER[0][s], NW, stride=2 * SLOTS), :],
            numbers[pl.ds(ORDER[1][s], NW, stride=2 * SLOTS), :],
        )
        for t in range(TILES):
            hot[s * NW : (s + 1) * NW, t * 128 : (t + 1) * 128] = onehot(
                mine == waves[:, t * 128 : (t + 1) * 128]
            )


def remote(src, dst, send_sem, recv_sem, device):
    return pltpu.make_async_remote_copy(
        src_ref=src, dst_ref=dst, send_sem=send_sem, recv_sem=recv_sem,
        device_id=device, device_id_type=MESH,
    )


def split(value):
    high = value.astype(BF16)
    return high, (value - high.astype(F32)).astype(BF16)


def product_of_parts(value, high, low):
    one, two = split(value)
    return jnp.dot(
        jnp.concatenate([one, two], axis=1),
        jnp.concatenate([high, high], axis=0),
        preferred_element_type=F32,
    ) + jnp.dot(one, low, preferred_element_type=F32)


def kernel(
    waves_ref, start_ref, pressure_ref, depths_ref, modes_ref, project_ref, heat_ref,
    x_ref, slots_ref, lats_ref, cosine_ref, logsin_ref, weight_ref,
    grid_mine_ref, grid_other_ref, state_mine_ref, state_other_ref,
    other, hot, rows, wide, send, land, send_back, land_back,
    coef_v, coef_s, table, block, folded_in, folds, spec, turned, gathered, north_south,
    ns_rows, numbers, lat_rows, lat_late, where, hot_rows, state_half, state_land, left, half, half_land,
    round_two, coef_sem, pair_send, pair_recv, own_sem, send_sem, recv_sem,
    state_send, state_recv, own_back_sem, send_back_sem, recv_back_sem, half_send, half_recv,
):
    wave, core = lax.axis_index("wave"), lax.axis_index("lev")
    partner = (wave, 1 - core)
    lane = iota((1, 128), 1)

    depth_at, plane_at = lax.div(wave, 16), lax.rem(wave, 16)
    barrier = pltpu.get_barrier_semaphore()

    def greet_depth(i, _):
        there = lax.rem(depth_at + i, 8) * 16 + plane_at
        pl.semaphore_signal(barrier, inc=1, device_id=(there, core), device_id_type=MESH)
        return 0

    def in_plane(i):
        return depth_at * 16 + lax.rem(plane_at + i, 16)

    def greet_plane(i, _):
        pl.semaphore_signal(barrier, inc=1, device_id=(in_plane(i), core), device_id_type=MESH)
        return 0

    def pass_on(i, _):
        pl.semaphore_signal(round_two, inc=1, device_id=(in_plane(i), core), device_id_type=MESH)
        return 0

    pl.semaphore_signal(barrier, inc=1, device_id=partner, device_id_type=MESH)
    lax.fori_loop(1, 8, greet_depth, 0)
    lax.fori_loop(1, 16, greet_plane, 0)

    held = [
        jnp.where(
            core == 0,
            waves_ref[wave * 2 * SLOTS + ORDER[0][s]],
            waves_ref[wave * 2 * SLOTS + ORDER[1][s]],
        )
        for s in range(SLOTS)
    ]
    firsts = [held[0], held[2], held[4]]
    seconds = [held[1], held[3], 0]
    begins = [(WAVES - firsts[c] + 15) // 16 * 16 for c in range(2)] + [CHAIN + 16]

    j = iota((8, PAD), 1)
    row = iota((8, PAD), 0)

    def per_chain(values):
        which = row % 4
        return jnp.where(which == 0, values[0], jnp.where(which == 1, values[1], values[2]))

    begin = per_chain(begins)
    second = j >= begin
    order = jnp.where(second, per_chain(seconds), per_chain(firsts))
    k = jnp.where(second, j - begin, j)
    n = (order + k).astype(F32)
    m = order.astype(F32)
    ok = (k >= 1) & (order + k < WAVES)
    grow = jnp.sqrt((4.0 * n * n - 1.0) / jnp.where(ok, n * n - m * m, 1.0))
    less = n - 1.0
    damp = jnp.sqrt(
        jnp.where(ok, jnp.maximum(less * less - m * m, 0.0), 0.0)
        / jnp.where(ok & (less > 0.0), 4.0 * less * less - 1.0, 1.0)
    )
    coef = jnp.where(ok, jnp.where(row < 4, grow, grow * damp), 0.0)
    coef_v[...] = coef
    coef_copy = pltpu.make_async_copy(coef_v, coef_s, coef_sem)
    coef_copy.start()

    columns_of(slots_ref, WAVES // 128, numbers)
    slot_onehot(core, numbers, hot)
    columns_of(lats_ref, NLAT // 128, numbers)

    pl.semaphore_wait(barrier, 7 + 15 + 1)
    lax.fori_loop(1, 16, pass_on, 0)
    pair = remote(x_ref, other, pair_send, pair_recv, partner)
    pair.start()

    def place(ref, side):
        for f in range(8):
            rows[side, f * PARTS : f * PARTS + ROWS, :] = ref[f].astype(F32)

    rows[...] = jnp.zeros((2, 8 * PARTS, WAVES), F32)
    place(x_ref, core)
    for w in range(NW):
        last = numbers[w * ROWS + 16 : w * ROWS + 20, :]
        lat_rows[w // 4, w % 4] = numbers[w * ROWS : w * ROWS + 16, :]
        lat_late[w // 4, w % 4] = jnp.concatenate([last, last], axis=0)
    lat_line = jnp.concatenate(
        [
            jnp.transpose(lat_rows[q * 2 : q * 2 + 2].reshape(128, 128))[0:1, :]
            for q in range(NW // 8)
        ]
        + [
            jnp.transpose(lat_late[q * 4 : q * 4 + 4].reshape(128, 128))[0:1, :]
            for q in range(NW // 16)
        ],
        axis=1,
    ).astype(jnp.int32)
    mirror_line = jnp.minimum(lat_line, NLAT - 1 - lat_line)

    cosine = [cosine_ref[0:8, :]] * 3 + [cosine_ref[8:16, :]]
    logsin = [logsin_ref[0:8, :]] * 3 + [logsin_ref[8:16, :]]
    sub = iota((8, 128), 0)

    def spread_rows(values):
        mixed = jnp.where(sub < 2, values[0], jnp.where(sub < 4, values[1], values[2]))
        return [values[0], values[1], values[2], mixed]

    def make(b, carry):
        current, former, scale = carry
        at_begin = [b * 16 == begins[c] for c in range(3)]
        wave_number = [
            jnp.where(at_begin[c], seconds[c], firsts[c]) for c in range(3)
        ]
        base = spread_rows([start_ref[w] for w in wave_number])
        degree = spread_rows([w.astype(F32) for w in wave_number])
        reset = spread_rows(
            [jnp.where((b == 0) | at_begin[c], 1.0, 0.0) for c in range(3)]
        )
        next_current, next_former, next_scale, factor = [], [], [], []
        for v in range(4):
            size = jnp.maximum(
                jnp.maximum(jnp.abs(current[v]), jnp.abs(former[v])), 1e-30
            )
            inverse = 1.0 / size
            again = reset[v] > 0.5
            if v < 3:
                again = jnp.broadcast_to(reset[v], (8, 128)) > 0.5
            next_current.append(jnp.where(again, 1.0, current[v] * inverse))
            next_former.append(jnp.where(again, 0.0, former[v] * inverse))
            next_scale.append(
                jnp.where(again, base[v] + degree[v] * logsin[v], scale[v] + jnp.log(size))
            )
            factor.append(jnp.exp(next_scale[v]))
        current, former = next_current, next_former
        for o in range(16):
            for v in range(4):
                block[pl.ds(v * 8 * STRIDE + o, 8, stride=STRIDE), :] = current[v] * factor[v]
            at = b * 16 + o + 1
            grow = spread_rows([coef_s[c, at] for c in range(3)])
            damp = spread_rows([coef_s[4 + c, at] for c in range(3)])
            following = [
                (cosine[v] * grow[v]) * current[v] - damp[v] * former[v] for v in range(4)
            ]
            former, current = current, following
        at = pl.multiple_of(b * 16, 16)
        for c in range(3):
            for t in range(TILES):
                line = c * 8 + t if t < 8 else 24 + 2 * c + t - 8
                table[c, pl.ds(at, 16), t * 128 : (t + 1) * 128] = block[
                    line * STRIDE : line * STRIDE + 16, :
                ].astype(BF16)
        return (tuple(current), tuple(former), tuple(next_scale))

    coef_copy.wait()
    zeros = tuple(jnp.zeros((8, 128), F32) for _ in range(4))
    carry = lax.fori_loop(0, EARLY, make, (zeros, zeros, zeros))

    pair.wait()
    place(other, 1 - core)
    arranged = lax.dot_general(
        rows[...].reshape(16 * PARTS, WAVES).astype(BF16),
        hot[...],
        (((1,), (1,)), ((), ())),
        preferred_element_type=F32,
    )
    for s in range(SLOTS):
        gathered[s] = arranged[:, s * NW : (s + 1) * NW]
    ahead = lane < 80

    def one_row(r):
        return jnp.transpose(
            jnp.concatenate(
                [
                    gathered[s, pl.ds(r, 16, stride=PARTS), :]
                    for s in range(SLOTS)
                ]
                + [jnp.zeros((48, NW), F32)],
                axis=0,
            )
        )

    for r in range(4):
        last = one_row(16 + r)
        wide[pl.ds(r, NW, stride=STRIDE), :] = jnp.where(
            ahead, one_row(r), pltpu.roll(last, 80, 1)
        )
        wide[pl.ds(4 + r, NW, stride=STRIDE), :] = jnp.where(
            ahead, one_row(4 + r), pltpu.roll(last, 32, 1)
        )
    for r in range(8, 16):
        wide[pl.ds(r, NW, stride=STRIDE), :] = one_row(r)
    for w in range(NW):
        send[w] = wide[w * STRIDE : w * STRIDE + 16, :].astype(BF16)
    pl.semaphore_wait(round_two, 15)
    own = pltpu.make_async_copy(send.at[wave], land.at[wave], own_sem)
    own.start()

    def send_to(step, _):
        offset = lax.rem(step, 8) * 16 + lax.div(step, 8)
        target = lax.rem(wave + offset, NW)
        remote(send.at[target], land.at[wave], send_sem, recv_sem, (target, core)).start()
        return 0

    lax.fori_loop(1, NW, send_to, 0)
    lax.fori_loop(EARLY, BLOCKS, make, carry)

    def where_from(t, _):
        at = pl.multiple_of(t * 128, 128)
        where[pl.ds(at, 128), :] = onehot(mirror_line == iota((128, KROWS), 0) + t * 128)
        return 0

    lax.fori_loop(0, TILES, where_from, 0)

    latitudes = iota((1, HEMI), 1).astype(F32)

    def lats_at(x):
        return jnp.concatenate(
            [lat_rows[:, x].reshape(512, 128), lat_late[:, x].reshape(256, 128)], axis=0
        )

    def where_to(x, _):
        lat = lats_at(x)
        mirror = jnp.minimum(lat, float(NLAT - 1) - lat)
        for t in range(TILES):
            hot_rows[x, :, t * 128 : (t + 1) * 128] = onehot(
                mirror == latitudes[:, t * 128 : (t + 1) * 128]
            )
        return 0

    lax.fori_loop(0, 4, where_to, 0)

    chain_of = lane // 32

    def lanes(values):
        return jnp.where(chain_of == 0, values[0], jnp.where(chain_of == 1, values[1], values[2]))

    is_second = (lane // 16) % 2 == 1
    lane_begin = lanes(begins)
    offset = jnp.where(is_second, lanes(seconds) - lane_begin, lanes(firsts))
    level = (lane // 8) % 2 * 2 + lane % 2
    field = (lane // 2) % 2
    depth = jnp.zeros((1, 128), F32)
    for a in range(4):
        depth = jnp.where(level == a, depths_ref[a], depth)
    across, down = iota((128, 128), 1), iota((128, 128), 0)
    same = (across // 16 == down // 16) & ((across // 4) % 2 == (down // 4) % 2)
    level_to, level_from = (across // 8) % 2 * 2 + across % 2, (down // 8) % 2 * 2 + down % 2
    field_to, field_from = (across // 2) % 2, (down // 2) % 2

    def matrix(entry, to, of):
        total = jnp.zeros((128, 128), F32)
        for a in range(4):
            for b in range(4):
                total = jnp.where((level_to == a) & (level_from == b), entry(a, b), total)
        return jnp.where(same & (field_to == to) & (field_from == of), total, 0.0)

    def product(one, two):
        return lambda a, b: sum(one[a, e] * two[e, b] for e in range(4))

    first_matrix = jnp.concatenate(
        [
            matrix(lambda a, b: project_ref[a, b], 0, 0),
            matrix(product(project_ref, pressure_ref), 0, 1),
        ],
        axis=1,
    )
    second_matrix = matrix(lambda a, b: modes_ref[a, b], 0, 0) - matrix(
        product(heat_ref, modes_ref), 1, 0
    )
    first_parts, second_parts = split(first_matrix), split(second_matrix)
    turned[:, CHAIN - 16 : PAD] = jnp.zeros((128, PAD - CHAIN + 16), F32)
    spec[CHAIN - 16 : PAD, :] = jnp.zeros((PAD - CHAIN + 16, 128), F32)
    ns_rows[:, 96:128, :] = jnp.zeros((2, 32, HEMI), F32)

    own.wait()
    all_but_one = pl.ds(0, NW - 1)
    pltpu.make_async_copy(send.at[all_but_one], land.at[all_but_one], send_sem).wait()
    pltpu.make_async_copy(send.at[all_but_one], land.at[all_but_one], recv_sem).wait()

    received = land[...].astype(F32)
    sub = iota((NW, 8, 128), 1)
    lanes_of = iota((NW, 8, 128), 2)
    tops = received[:, 0:8, :].reshape(NW * 8, 128)
    three = pltpu.roll(tops, 48, 1).reshape(NW, 8, 128)
    two = pltpu.roll(tops, 96, 1).reshape(NW, 8, 128)
    late = jnp.where(
        sub < 4,
        jnp.where(lanes_of < 48, three, 0.0),
        jnp.where((lanes_of >= 48) & (lanes_of < 80), two, 0.0),
    ).reshape(NW * 8, 128)
    early = jnp.where(ahead, received.reshape(NW * 16, 128), 0.0)
    for at, part, lats in ((0, early, lat_rows), (NW * 16, late, lat_late)):
        end = at + part.shape[0]
        northern = lats[...].reshape(part.shape) < float(HEMI)
        folded_in[at:end, 0:128] = part.astype(BF16)
        folded_in[at:end, 128:256] = jnp.where(northern, part, -part).astype(BF16)

    def fold(t, _):
        at = pl.multiple_of(t * 256, 256)
        folds[pl.ds(at, 256), :] = jnp.dot(
            where[pl.ds(at, 256), :], folded_in[...], preferred_element_type=F32
        )
        return 0

    lax.fori_loop(0, HEMI // 256, fold, 0)
    for t in range(TILES):
        north_south[t * 128 : (t + 1) * 128, :] = (
            folds[t * 128 : (t + 1) * 128, :] * weight_ref[:, t : t + 1]
        ).astype(BF16)

    step_rows = CHAIN // 3

    def solve(q, _):
        at = pl.multiple_of(q * step_rows, 16)
        j = iota((step_rows, 128), 0) + at
        parts = []
        for c in range(3):
            both = jnp.dot(
                table[c, pl.ds(at, step_rows), :], north_south[...], preferred_element_type=F32
            )
            parts.append(jnp.where(j % 2 == 0, both[:, 0:128], both[:, 128:256]))
        spectrum = jnp.where(chain_of == 0, parts[0], jnp.where(chain_of == 1, parts[1], parts[2]))
        spectrum = jnp.where((j >= lane_begin) == is_second, spectrum, 0.0)
        n = (j + offset).astype(F32)
        coupling = n * (n + 1.0) * (1.0 / float(WAVES * WAVES))
        mixed = product_of_parts(spectrum, *first_parts)
        scaled = (mixed[:, 0:128] + coupling * mixed[:, 128:256]) / (1.0 + coupling * depth)
        updated = product_of_parts(scaled, *second_parts) + jnp.where(field == 1, spectrum, 0.0)
        spec[pl.ds(at, step_rows), :] = updated.astype(BF16).astype(F32)
        return 0

    lax.fori_loop(0, 3, solve, 0)
    for t in range(PAD // 128):
        turned[:, t * 128 : (t + 1) * 128] = jnp.transpose(spec[t * 128 : (t + 1) * 128, :])
    for s in range(SLOTS):
        for v in range(2):
            value = turned[s * 16 + v * 8 : s * 16 + v * 8 + 8, :]
            if s % 2 == 1:
                for bit in range(4, 11):
                    moved = pltpu.roll(value, PAD - (1 << bit) % PAD, 1)
                    value = jnp.where((begins[s // 2] >> bit) % 2 == 1, moved, value)
            state_half[v, s] = value[:, 0:WAVES].astype(BF16)
    state_copy = remote(
        state_half.at[1 - core], state_land, state_send, state_recv, partner
    )
    state_copy.start()

    even = iota((1, CHAIN), 1) % 2 == 0
    inverse_scale = 1.0 / math.sqrt(WAVES)
    for c in range(3):
        state = turned[c * 32 : c * 32 + 32, 0:CHAIN]
        both_parities = jnp.concatenate(
            [jnp.where(even, state, 0.0), jnp.where(even, 0.0, state)], axis=0
        ).astype(BF16)
        for t in range(HEMI // 256):
            both = jnp.dot(
                both_parities, table[c, :, t * 256 : (t + 1) * 256], preferred_element_type=F32
            )
            sym, anti = both[0:32], both[32:64]
            ns_rows[0, c * 32 : c * 32 + 32, t * 256 : (t + 1) * 256] = (sym + anti) * inverse_scale
            ns_rows[1, c * 32 : c * 32 + 32, t * 256 : (t + 1) * 256] = (sym - anti) * inverse_scale
    for u in range(2):
        for t in range(TILES):
            north_south[t * 128 : (t + 1) * 128, u * 128 : (u + 1) * 128] = jnp.transpose(
                ns_rows[u, :, t * 128 : (t + 1) * 128]
            ).astype(BF16)

    own_back = pltpu.make_async_copy(send_back.at[wave], land_back.at[wave], own_back_sem)
    sub = iota((32, 8, 128), 1)
    for g in range(4):
        x = lax.rem(wave + g, 4)
        lat = lats_at(x)
        both = jnp.dot(hot_rows[x], north_south[...], preferred_element_type=F32)
        part = jnp.where(lat < float(HEMI), both[:, 0:128], both[:, 128:256])
        late = part[512:768]
        late = jnp.where(
            sub < 4,
            pltpu.roll(late, 80, 1).reshape(32, 8, 128),
            pltpu.roll(late, 32, 1).reshape(32, 8, 128),
        )
        tile = part[0:512].reshape(32, 16, 128)
        tile = jnp.concatenate(
            [jnp.where(ahead.reshape(1, 1, 128), tile[:, 0:8], late), tile[:, 8:16]], axis=1
        ).astype(BF16)
        for i in range(32):
            send_back[i * 4 + x] = tile[i]

        def give(i, _, x=x):
            offset = lax.rem(i, 8) * 4 + lax.div(i, 8)
            target = lax.rem(lax.div(wave, 4) + offset, 32) * 4 + x
            remote(
                send_back.at[target], land_back.at[wave], send_back_sem, recv_back_sem,
                (target, core),
            ).start()
            return 0

        if g == 0:
            own_back.start()
        lax.fori_loop(1 if g == 0 else 0, 32, give, 0)

    state_copy.wait()
    for s in range(SLOTS):
        mine = jnp.where(core == 0, state_half[0, s].astype(F32), state_half[1, s].astype(F32))
        theirs = state_land[s].astype(F32)
        none = jnp.zeros_like(mine)
        state_mine_ref[ORDER[0][s]] = jnp.where(core == 0, mine, none).astype(BF16)
        state_mine_ref[ORDER[1][s]] = jnp.where(core == 0, none, mine).astype(BF16)
        state_other_ref[ORDER[0][s]] = jnp.where(core == 0, none, theirs).astype(BF16)
        state_other_ref[ORDER[1][s]] = jnp.where(core == 0, theirs, none).astype(BF16)
    own_back.wait()
    pltpu.make_async_copy(
        send_back.at[all_but_one], land_back.at[all_but_one], send_back_sem
    ).wait()
    pltpu.make_async_copy(
        send_back.at[all_but_one], land_back.at[all_but_one], recv_back_sem
    ).wait()

    for w in range(NW):
        wide[w * STRIDE : w * STRIDE + 16, :] = land_back[w].astype(F32)
    for r in range(16):
        value = jnp.transpose(wide[pl.ds(r, NW, stride=STRIDE), :])
        blocks = [(r, s) for s in range(SLOTS)]
        if r < 4:
            blocks += [(16 + r, s) for s in range(3)]
        elif r < 8:
            blocks += [(12 + r, s) for s in range(3, SLOTS)]
        for q, (at, s) in enumerate(blocks):
            for v in range(2):
                left[v, s, pl.ds(at, 8, stride=PARTS), :] = value[
                    q * 16 + v * 8 : q * 16 + v * 8 + 8
                ]

    def columns(side, ref):
        value = jnp.dot(
            jnp.concatenate([left[side, s].astype(BF16) for s in range(SLOTS)], axis=1),
            hot[...],
            preferred_element_type=F32,
        )
        for f in range(8):
            ref[f] = value[f * PARTS : f * PARTS + ROWS].astype(BF16)

    columns(1 - core, half)
    half_copy = remote(half, half_land, half_send, half_recv, partner)
    half_copy.start()
    columns(core, grid_mine_ref)
    half_copy.wait()
    grid_other_ref[...] = half_land[...]


def vmem():
    return pl.BlockSpec(memory_space=pltpu.VMEM)


def smem():
    return pl.BlockSpec(memory_space=pltpu.SMEM)


def run(wave_slots, matrices, x, slots, lats):
    cosine, logsin, weight, start = constants()
    pressure, depths, modes, project, heat = matrices
    dma = pltpu.SemaphoreType.DMA
    return pl.pallas_call(
        kernel,
        out_shape=(
            jax.ShapeDtypeStruct((8, ROWS, WAVES), BF16),
            jax.ShapeDtypeStruct((8, ROWS, WAVES), BF16),
            jax.ShapeDtypeStruct((2 * SLOTS, 8, WAVES), BF16),
            jax.ShapeDtypeStruct((2 * SLOTS, 8, WAVES), BF16),
        ),
        in_specs=[smem()] * 7 + [vmem()] * 6,
        out_specs=(vmem(), vmem(), vmem(), vmem()),
        scratch_shapes=[
            pltpu.VMEM((8, ROWS, WAVES), BF16),
            pltpu.VMEM((SLOTS * NW, WAVES), BF16),
            pltpu.VMEM((2, 8 * PARTS, WAVES), F32),
            pltpu.VMEM((NW * STRIDE, 128), F32),
            pltpu.VMEM((NW, 16, 128), BF16),
            pltpu.VMEM((NW, 16, 128), BF16),
            pltpu.VMEM((NW, 16, 128), BF16),
            pltpu.VMEM((NW, 16, 128), BF16),
            pltpu.VMEM((8, PAD), F32),
            pltpu.SMEM((8, PAD), F32),
            pltpu.VMEM((3, CHAIN, HEMI), BF16),
            pltpu.VMEM((32 * STRIDE, 128), F32),
            pltpu.VMEM((KROWS, 256), BF16),
            pltpu.VMEM((HEMI, 256), F32),
            pltpu.VMEM((PAD, 128), F32),
            pltpu.VMEM((128, PAD), F32),
            pltpu.VMEM((SLOTS, 16 * PARTS, NW), F32),
            pltpu.VMEM((HEMI, 256), BF16),
            pltpu.VMEM((2, 128, HEMI), F32),
            pltpu.VMEM((NLAT, 128), F32),
            pltpu.VMEM((32, 4, 16, 128), F32),
            pltpu.VMEM((32, 4, 8, 128), F32),
            pltpu.VMEM((HEMI, KROWS), BF16),
            pltpu.VMEM((4, KROWS // 4, HEMI), BF16),
            pltpu.VMEM((2, SLOTS, 8, WAVES), BF16),
            pltpu.VMEM((SLOTS, 8, WAVES), BF16),
            pltpu.VMEM((2, SLOTS, 8 * PARTS, NW), F32),
            pltpu.VMEM((8, ROWS, WAVES), BF16),
            pltpu.VMEM((8, ROWS, WAVES), BF16),
            pltpu.SemaphoreType.REGULAR,
        ]
        + [dma] * 13,
        compiler_params=pltpu.CompilerParams(
            vmem_limit_bytes=VMEM, has_side_effects=True, collective_id=1
        ),
    )(
        wave_slots, jnp.asarray(start), pressure, depths, modes, project, heat,
        x, slots, lats, jnp.asarray(cosine), jnp.asarray(logsin), jnp.asarray(weight),
    )


def body(
    fourier,
    lat_rows,
    wave_slots,
    pressure_balance_operator,
    depths,
    vertical_modes,
    mode_projection,
    heat_link_operator,
):
    matrices = (
        pressure_balance_operator, depths, vertical_modes, mode_projection, heat_link_operator,
    )
    grid, grid_other, state, state_other = run(
        wave_slots,
        matrices,
        fourier.reshape(8, ROWS, WAVES),
        wave_slots.reshape(WAVES // 128, 128),
        lat_rows.reshape(NLAT // 128, 128),
    )
    return (
        (state + state_other).reshape(2 * SLOTS, 2, 2, 2, WAVES),
        (grid + grid_other).reshape(2, 2, 2, ROWS, WAVES),
    )


def solution(mesh):
    in_specs = (P(None, None, "lev", "wave", None), P(), P(), P(), P(), P(), P(), P())
    out_specs = (P("wave", None, None, "lev", None), P(None, None, "lev", "wave", None))
    return jax.shard_map(body, mesh=mesh, in_specs=in_specs, out_specs=out_specs, check_vma=False)
```
